32 devices in a mesh: clips: 2 (over x), pix: 2 (over core), frame: 8 (over z, y).
Axes of the slice: x: 2, y: 2, z: 4, core: 2. Of those that a mesh axis runs over, the one named last changes fastest.
Arguments:
- stream: bfloat16 [2, 16, 384, 1152], P(None, ('clips', 'frame'), 'pix'), parts along dimension 1, may hold values from -8 to 8
- spatial_qkv: bfloat16 [2, 3, 16, 384, 1152], P(None, None, ('clips', 'frame'), 'pix'), parts along dimension 2, as said below
- out_weight: bfloat16 [1152, 1152], P(None, 'frame'), may hold values from -0.1875 to 0.1875
- qkv_weight: bfloat16 [1152, 3456], P(None, 'frame')
- mod_table: float32 [3, 2, 1152], replicated, may hold values from -3 to 3
- timestep: int32 [2], P('clips'), parts along dimension 0, may hold values from 0 to 999
Outputs:
- residual: float32 [2, 16, 384, 1152], P(None, ('clips', 'frame'), 'pix'), parts along dimension 1
- temporal: float32 [2, 16, 384, 1152], P(None, ('clips', 'frame'), 'pix'), parts along dimension 1
The draws below stay inside these ranges and needn't reach their ends.
There are 2 independent parts, one for each index of `clips`. The reference program is written for one: setup_inputs(seed, part) draws one part's arguments, and reference() takes and returns one part's arrays. A program takes and returns all parts, laid end to end along the dimension named above; an argument that names none is the same for every part. Nothing has to cross between parts.
Inputs may be any that keep to these rules, and one draw needn't show every extreme that they name: `spatial_qkv`: Queries, keys and values of the spatial attention, primal in the first index and tangent in the second.
All inputs are finite; a program needn't handle non-finite values.
Results may differ from the reference program's by a relative error of at most 0.0097.
Values may be sent and summed in bfloat16 or wider, within the bound.
A program may use at most 128 MiB of HBM per device.

```python
import math
import jax
import jax.numpy as jnp
from jax import lax

D = 1152
HEAD_DIM = 72
FRAMES = 8
POSITIONS = 384


def draw_spatial_qkv(key, part):
    shape = (2, 3, FRAMES, POSITIONS, D)
    drawn = jnp.clip(jax.random.normal(key, shape, jnp.float32), -6.0, 6.0)
    return drawn.astype(jnp.bfloat16)


def draw_stream(key, part):
    shape = (2, FRAMES, POSITIONS, D)
    drawn = jnp.clip(jax.random.normal(key, shape, jnp.float32), -6.0, 6.0)
    return drawn.astype(jnp.bfloat16)


def draw_qkv_weight(key, part):
    scale_factor = 1.0 / D ** 0.5
    shape = (D, 3 * D)
    drawn = jnp.clip(jax.random.normal(key, shape, jnp.float32), -6.0, 6.0) * scale_factor
    return drawn.astype(jnp.bfloat16)


def shard_levels(stream_key, extent, shards, least, top_value):
    gain, own = 1.0, jax.random.fold_in(stream_key, 6)
    for position, parts in shards:
        heights = jnp.exp(jax.random.uniform(jax.random.fold_in(own, position), (parts,), jnp.float32, least / len(shards), top_value / len(shards)))
        gain = gain * jnp.repeat(heights, extent[position] // parts).reshape([-1 if axis == position else 1 for axis in range(len(extent))])
    return gain


def scatter_about(stream_key, shape, scale, reach, shards=(), kind=jnp.bfloat16):
    loudness = shard_levels(stream_key, shape, shards, -0.22, 0.18) if shards else 1.0
    values = jax.random.normal(stream_key, shape, jnp.float32) * scale * loudness
    return jnp.minimum(jnp.maximum(values, -reach), reach).astype(kind)


def setup_inputs(seed: int = 0, part: int = 0) -> dict:
    splits = jax.random.split(jax.random.key(seed), 7)
    own_keys = jax.random.split(jax.random.fold_in(splits[6], part), 7)
    return {
        "stream": draw_stream(jax.random.fold_in(jax.random.fold_in(splits[6], part), 71), part),
        "spatial_qkv": draw_spatial_qkv(jax.random.fold_in(jax.random.fold_in(splits[6], part), 71), part),
        "out_weight": scatter_about(splits[2], (D, D), D ** -0.5, 0.1875, ((1, 8),)),
        "qkv_weight": draw_qkv_weight(jax.random.fold_in(splits[6], 71), part),
        "mod_table": scatter_about(splits[4], (3, 2, D), 0.6, 3.0, (), jnp.float32),
        "timestep": jax.random.randint(own_keys[5], (1,), 0, 1000).astype(jnp.int32),
    }


def modulation(mod_table, timestep):
    width = mod_table.shape[-1]
    frequency = jnp.exp(-math.log(10.0) * jnp.arange(width).astype(jnp.float32) / width)
    time_value = timestep[0].astype(jnp.float32) * (math.pi / 1000.0)
    mod_value = mod_table[:, 0] + mod_table[:, 1] * jnp.cos(frequency * time_value)
    mod_slope = -mod_table[:, 1] * frequency * jnp.sin(frequency * time_value)
    return (mod_value, mod_slope)

def attend(query, keys, values, query_dot, keys_dot, values_dot):
    scale = 1.0 / math.sqrt(query.shape[-1])
    to_float = lambda array: array.astype(jnp.float32)
    scores = jnp.einsum('blhe,bmhe->bhlm', to_float(query), to_float(keys)) * scale
    scores_dot = (jnp.einsum('blhe,bmhe->bhlm', to_float(query_dot), to_float(keys)) + jnp.einsum('blhe,bmhe->bhlm', to_float(query), to_float(keys_dot))) * scale
    top_score = lax.optimization_barrier(jnp.max(scores, axis=-1, keepdims=True))
    expo = jnp.exp(scores - top_score)
    probs = expo / lax.optimization_barrier(jnp.sum(expo, axis=-1, keepdims=True))
    probs_low = probs.astype(jnp.bfloat16)
    output = jnp.einsum('bhlm,bmhe->blhe', to_float(probs_low), to_float(values))
    row_total = lax.optimization_barrier(jnp.sum(probs * scores_dot, axis=-1, keepdims=True))
    weighted = probs * (scores_dot - row_total)
    weighted_low = weighted.astype(jnp.bfloat16)
    output_dot = jnp.einsum('bhlm,bmhe->blhe', to_float(weighted_low), to_float(values)) + jnp.einsum('bhlm,bmhe->blhe', to_float(probs_low), to_float(values_dot))
    return (output, output_dot)

def reference(stream, spatial_qkv, out_weight, qkv_weight, mod_table, timestep):
    frames_all = stream.shape[1]
    places = stream.shape[2]
    width = stream.shape[3]
    heads_all = width // HEAD_DIM

    def per_frame(index):
        block = lax.dynamic_index_in_dim(spatial_qkv, index, 2, keepdims=False)
        shaped = block.reshape(2, 3, 1, places, heads_all, HEAD_DIM)
        output, output_dot = attend(shaped[0, 0], shaped[0, 1], shaped[0, 2], shaped[1, 0], shaped[1, 1], shaped[1, 2])
        return jnp.stack([output, output_dot]).reshape(2, places, width).astype(jnp.bfloat16)
    spatial = lax.map(per_frame, jnp.arange(frames_all))
    spatial = jnp.moveaxis(spatial, 0, 1)
    mod_value, mod_slope = modulation(mod_table, timestep)
    projected = jnp.dot(spatial.reshape(-1, width), out_weight, preferred_element_type=jnp.float32).reshape(2, frames_all, places, width)
    primal_in = stream[0].astype(jnp.float32)
    tangent_in = stream[1].astype(jnp.float32)
    hidden = primal_in + mod_value[0] * projected[0]
    hidden_dot = tangent_in + mod_slope[0] * projected[0] + mod_value[0] * projected[1]
    centered = hidden - lax.optimization_barrier(jnp.mean(hidden, axis=-1, keepdims=True))
    inv_scale = lax.rsqrt(lax.optimization_barrier(jnp.mean(centered * centered, axis=-1, keepdims=True)) + 1e-06)
    normed = centered * inv_scale
    normed_dot = (hidden_dot - lax.optimization_barrier(jnp.mean(hidden_dot, axis=-1, keepdims=True)) - normed * lax.optimization_barrier(jnp.mean(normed * hidden_dot, axis=-1, keepdims=True))) * inv_scale
    modulated = normed * (1.0 + mod_value[2]) + mod_value[1]
    modulated_dot = normed_dot * (1.0 + mod_value[2]) + normed * mod_slope[2] + mod_slope[1]
    modulated_low = jnp.stack([modulated, modulated_dot]).astype(jnp.bfloat16)
    projected_qkv = jnp.dot(modulated_low.reshape(-1, width), qkv_weight, preferred_element_type=jnp.float32).astype(jnp.bfloat16)
    projected_qkv = projected_qkv.reshape(2, frames_all, places, 3, heads_all, HEAD_DIM)
    arranged = jnp.transpose(projected_qkv, (0, 3, 2, 1, 4, 5))
    output, output_dot = attend(arranged[0, 0], arranged[0, 1], arranged[0, 2], arranged[1, 0], arranged[1, 1], arranged[1, 2])
    temporal = jnp.transpose(jnp.stack([output, output_dot]), (0, 2, 1, 3, 4)).reshape(2, frames_all, places, width)
    residual = jnp.stack([hidden, hidden_dot])
    return (residual, temporal)
```

```python
import functools
import math

import jax
import jax.numpy as jnp
from jax import lax
from jax.experimental import pallas as pl
from jax.experimental.pallas import tpu as pltpu
from jax.sharding import PartitionSpec as P

HEAD_DIM = 72
LANES = 128
TILE = 384


def modulation(mod_table, timestep):
    width = mod_table.shape[-1]
    frequency = jnp.exp(-math.log(10.0) * jnp.arange(width).astype(jnp.float32) / width)
    time_value = timestep[0].astype(jnp.float32) * (math.pi / 1000.0)
    mod_value = mod_table[:, 0] + mod_table[:, 1] * jnp.cos(frequency * time_value)
    mod_slope = -mod_table[:, 1] * frequency * jnp.sin(frequency * time_value)
    return (mod_value, mod_slope)


def attend_group(inputs):
    query, keys, values, query_dot, keys_dot, values_dot = inputs
    scale = 1.0 / math.sqrt(query.shape[-1])
    scores = jnp.einsum("blhe,bmhe->bhlm", query, keys, preferred_element_type=jnp.float32) * scale
    scores_dot = (
        jnp.einsum("blhe,bmhe->bhlm", query_dot, keys, preferred_element_type=jnp.float32)
        + jnp.einsum("blhe,bmhe->bhlm", query, keys_dot, preferred_element_type=jnp.float32)
    ) * scale
    top_score = jnp.max(scores, axis=-1, keepdims=True)
    expo = jnp.exp(scores - top_score)
    probs = expo / jnp.sum(expo, axis=-1, keepdims=True)
    probs_low = probs.astype(jnp.bfloat16)
    output = jnp.einsum("bhlm,bmhe->blhe", probs_low, values, preferred_element_type=jnp.float32)
    row_total = jnp.sum(probs * scores_dot, axis=-1, keepdims=True)
    weighted = probs * (scores_dot - row_total)
    weighted_low = weighted.astype(jnp.bfloat16)
    output_dot = jnp.einsum(
        "bhlm,bmhe->blhe", weighted_low, values, preferred_element_type=jnp.float32
    ) + jnp.einsum("bhlm,bmhe->blhe", probs_low, values_dot, preferred_element_type=jnp.float32)
    return (output, output_dot)


def attend(stacked, group_size):
    batch, length, heads_all, head_size = stacked.shape[2:]
    groups = heads_all // group_size
    shaped = stacked.reshape(2, 3, batch, length, groups, group_size, head_size)
    shaped = jnp.transpose(shaped, (4, 0, 1, 2, 3, 5, 6))
    inputs = (
        shaped[:, 0, 0],
        shaped[:, 0, 1],
        shaped[:, 0, 2],
        shaped[:, 1, 0],
        shaped[:, 1, 1],
        shaped[:, 1, 2],
    )
    output, output_dot = lax.map(attend_group, inputs)
    joined = jnp.stack([output, output_dot], axis=1)
    joined = jnp.transpose(joined, (1, 2, 3, 0, 4, 5))
    return joined.reshape(2, batch, length, heads_all * head_size)


def per_device(stream, spatial_qkv, out_weight, qkv_weight, mod_table, timestep):
    frames_local = stream.shape[1]
    places = stream.shape[2]
    width = stream.shape[3]
    block = lax.all_to_all(spatial_qkv, "pix", split_axis=4, concat_axis=3, tiled=True)
    frames_here = block.shape[2]
    length = block.shape[3]
    channels = block.shape[4]
    shaped = block.reshape(2, 3, frames_here, length, channels // HEAD_DIM, HEAD_DIM)
    attended = attend(shaped, 1).astype(jnp.bfloat16)
    spatial = lax.all_to_all(attended, "pix", split_axis=2, concat_axis=3, tiled=True)
    flat_spatial = spatial.reshape(-1, width)
    projected = jnp.dot(
        flat_spatial,
        lax.all_gather(out_weight, "frame", axis=1, tiled=True),
        preferred_element_type=jnp.float32,
    )
    projected = projected.reshape(2, frames_local, places, width)
    mod_value, mod_slope = modulation(mod_table, timestep)
    primal_in = stream[0].astype(jnp.float32)
    tangent_in = stream[1].astype(jnp.float32)
    hidden = primal_in + mod_value[0] * projected[0]
    hidden_dot = tangent_in + mod_slope[0] * projected[0] + mod_value[0] * projected[1]
    centered = hidden - jnp.mean(hidden, axis=-1, keepdims=True)
    inv_scale = lax.rsqrt(jnp.mean(centered * centered, axis=-1, keepdims=True) + 1e-06)
    normed = centered * inv_scale
    normed_dot = (
        hidden_dot
        - jnp.mean(hidden_dot, axis=-1, keepdims=True)
        - normed * jnp.mean(normed * hidden_dot, axis=-1, keepdims=True)
    ) * inv_scale
    modulated = normed * (1.0 + mod_value[2]) + mod_value[1]
    modulated_dot = normed_dot * (1.0 + mod_value[2]) + normed * mod_slope[2] + mod_slope[1]
    modulated_low = jnp.stack([modulated, modulated_dot]).astype(jnp.bfloat16)
    moved_rows = lax.all_to_all(modulated_low, "frame", split_axis=2, concat_axis=1, tiled=True)
    frames_all = moved_rows.shape[1]
    sub_places = moved_rows.shape[2]
    flat_rows = moved_rows.reshape(-1, width)
    projected_qkv = (
        jnp.dot(
            flat_rows,
            lax.all_gather(qkv_weight, "frame", axis=1, tiled=True),
            preferred_element_type=jnp.float32,
        )
        .astype(jnp.bfloat16)
        .reshape(2, frames_all, sub_places, 3, width)
    )
    moved = jnp.transpose(projected_qkv, (0, 3, 1, 2, 4))
    frames_all = moved.shape[2]
    sub_places = moved.shape[3]
    arranged = jnp.transpose(moved, (0, 1, 3, 2, 4)).reshape(
        2, 3, sub_places, frames_all, width // HEAD_DIM, HEAD_DIM
    )
    attended = attend(arranged, width // HEAD_DIM)
    attended = jnp.transpose(attended, (0, 2, 1, 3))
    temporal = lax.all_to_all(attended, "frame", split_axis=1, concat_axis=2, tiled=True)
    residual = jnp.stack([hidden, hidden_dot])
    return (residual, temporal)


def lane_window(head):
    low = head * HEAD_DIM // LANES * LANES
    high = -(-(head * HEAD_DIM + HEAD_DIM) // LANES) * LANES
    return low, high


def head_mask(head, low, high):
    lane = lax.broadcasted_iota(jnp.int32, (1, high - low), 1) + low
    return (lane >= head * HEAD_DIM) & (lane < (head + 1) * HEAD_DIM)


def across(left, right):
    return lax.dot_general(left, right, (((1,), (1,)), ((), ())), preferred_element_type=jnp.float32)


def attend_head(mask, query, keys, values, query_dot, keys_dot, values_dot, allowed=None):
    scale = 1.0 / math.sqrt(HEAD_DIM)
    keep = mask.astype(jnp.float32).astype(jnp.bfloat16)
    rows = query.shape[0]
    query = query * keep
    query_dot = query_dot * keep
    both = across(jnp.concatenate([query, query_dot], axis=0), keys)
    scores = both[:rows] * scale
    scores_dot = (both[rows:] + across(query, keys_dot)) * scale
    if allowed is not None:
        scores = jnp.where(allowed, scores, -jnp.inf)
    expo = jnp.exp(scores - jnp.max(scores, axis=-1, keepdims=True))
    probs = expo * (1.0 / jnp.sum(expo, axis=-1, keepdims=True))
    weighted = probs * (scores_dot - jnp.sum(probs * scores_dot, axis=-1, keepdims=True))
    probs_low = probs.astype(jnp.bfloat16)
    stacked = jnp.concatenate([probs_low, weighted.astype(jnp.bfloat16)], axis=0)
    both = jnp.dot(stacked, values, preferred_element_type=jnp.float32)
    output_dot = both[rows:] + jnp.dot(probs_low, values_dot, preferred_element_type=jnp.float32)
    return both[:rows], output_dot


class LaneTiles:
    def __init__(self, heads):
        self.held = {}
        self.last = {}
        for head in range(heads):
            low, high = lane_window(head)
            for tile in range(low // LANES, high // LANES):
                self.last[tile] = head

    def add(self, head, mask, output, output_dot):
        low, high = lane_window(head)
        done = []
        for tile in range(low // LANES, high // LANES):
            part = slice(tile * LANES - low, (tile + 1) * LANES - low)
            here = mask[:, part]
            pair = (output[:, part], output_dot[:, part])
            if tile in self.held:
                pair = tuple(jnp.where(here, a, b) for a, b in zip(pair, self.held[tile]))
            self.held[tile] = pair
            if self.last[tile] == head:
                done.append((tile, self.held.pop(tile)))
        return done


def fused_kernel(
    n, spatial, stream, out_own, qkv_own, mod, residual, returned,
    peer_kv, out_all, qkv_all, attended, rows_send, rows_recv, qkv, back_send,
    kv_sem, own_sem, ring_send, ring_recv, core_send, core_recv, x_send, x_recv,
    xcore_send, xcore_recv, row_send_sem, row_recv_sem, back_send_sem, back_recv_sem,
):
    clip, core, me = lax.axis_index("clips"), lax.axis_index("pix"), lax.axis_index("frame")
    side = lax.rem(clip, 2)
    x_peer = clip + 1 - 2 * side
    places, width = stream.shape[2], stream.shape[3]
    part = places // n
    heads = width // HEAD_DIM
    half = n // 2

    depth_of = lambda frame: lax.div(frame, 2)
    row_of = lambda frame: lax.rem(frame, 2)
    place_of = lambda frame: depth_of(frame) * (1 - row_of(frame)) + (n - 1 - depth_of(frame)) * row_of(frame)

    def frame_at(place):
        later = lax.div(place, half)
        return (1 - later) * (2 * place) + later * (2 * (n - 1 - place) + 1)

    place = place_of(me)
    step_by = 1 - 2 * core
    behind = lambda steps: frame_at(lax.rem(place - steps * step_by + 2 * n, n))
    after = behind(-1)
    to_peer = {"pix": 1 - core}
    to_x = {"clips": x_peer}
    to_next = {"frame": after}

    barrier = pltpu.get_barrier_semaphore()
    for target in [to_peer, to_x] + [{"frame": lax.rem(me + k, n)} for k in range(1, n)]:
        pl.semaphore_signal(barrier, inc=1, device_id=target, device_id_type=pl.DeviceIdType.MESH)
    pl.semaphore_wait(barrier, n + 1)

    def remote(source, target, send, recv, device):
        return pltpu.make_async_remote_copy(
            src_ref=source, dst_ref=target, send_sem=send, recv_sem=recv,
            device_id=device, device_id_type=pl.DeviceIdType.MESH,
        )

    kv_copy = remote(spatial.at[:, 1:3, 0], peer_kv, kv_sem.at[0], kv_sem.at[1], to_peer)
    kv_copy.start()

    gathered = (out_all, qkv_all)
    owned = (out_own, qkv_own)
    sizes = tuple(ref.shape[0] for ref in owned)
    my_third = core + (1 - core) * 2 * side
    peer_third = (1 - core) + core * 2 * side
    x_third = 2 * (1 - side)

    def piece(which, frame, third):
        size = sizes[which] // 3
        return gathered[which].at[pl.ds(pl.multiple_of(frame * sizes[which] + third * size, 16), size)]

    def ring_copy(which, step):
        block = piece(which, behind(step - 1), my_third)
        if step == 1:
            size = sizes[which] // 3
            source = owned[which].at[pl.ds(pl.multiple_of(my_third * size, 16), size)]
        else:
            source = block
        return remote(source, block, ring_send.at[which, step], ring_recv.at[which, step], to_next)

    def arrives(block, recv):
        return remote(block, block, kv_sem.at[0], recv, to_peer)

    def core_copy(which, step):
        block = piece(which, behind(step), my_third)
        return remote(block, block, core_send.at[which, step], core_recv.at[which, step], to_peer)

    def x_copy(which, step):
        block = piece(which, behind(step), my_third)
        return remote(block, block, x_send.at[which, step], x_recv.at[which, step], to_x)

    def xcore_copy(which, step):
        block = piece(which, behind(step), x_third)
        return remote(block, block, xcore_send.at[which, step], xcore_recv.at[which, step], to_peer)

    def ring_step(which, step):
        arrives(piece(which, behind(step), my_third), ring_recv.at[which, step]).wait_recv()
        if step < n - 1:
            ring_copy(which, step + 1).start()

        @pl.when(core == 0)
        def _():
            x_copy(which, step).start()

        core_copy(which, step).start()

    def x_step(which, step):
        @pl.when(core == 0)
        def _():
            arrives(piece(which, behind(step), x_third), x_recv.at[which, step]).wait_recv()
            xcore_copy(which, step).start()

    def all_here(which):
        for step in range(1, n):
            other = frame_at(lax.rem(place + step * step_by + 2 * n, n))
            arrives(piece(which, other, peer_third), core_recv.at[which, step]).wait_recv()

        @pl.when(core == 1)
        def _():
            for step in range(1, n):
                other = frame_at(lax.rem(place + step * step_by + 2 * n, n))
                arrives(piece(which, other, x_third), xcore_recv.at[which, step]).wait_recv()

    own_copies = []
    for which in (0, 1):
        ring_copy(which, 1).start()
        whole = gathered[which].at[pl.ds(pl.multiple_of(me * sizes[which], 16), sizes[which])]
        own_copies.append(pltpu.make_async_copy(owned[which], whole, own_sem.at[which]))
        own_copies[-1].start()

    events = []
    for step in range(1, n):
        events.append((2.0 * step, ring_step, 0, step))
        events.append((2.0 * step + 2.0, x_step, 0, step))
        events.append((4.0 * step, ring_step, 1, step))
        events.append((4.0 * step + 3.0, x_step, 1, step))
    events.sort(key=lambda event: event[0])

    def serve(until):
        while events and events[0][0] <= until:
            _, act, which, step = events.pop(0)
            act(which, step)

    def serve_all(which):
        for event in [event for event in events if event[2] == which]:
            events.remove(event)
            event[1](event[2], event[3])

    kv_copy.wait_recv()
    tiles = LaneTiles(heads)
    for head in range(heads):
        low, high = lane_window(head)
        mask = head_mask(head, low, high)
        both = lambda t, j: jnp.concatenate([spatial[t, 1 + j, 0, :, low:high], peer_kv[t, j, :, low:high]], axis=0)
        output, output_dot = attend_head(
            mask, spatial[0, 0, 0, :, low:high], both(0, 0), both(0, 1),
            spatial[1, 0, 0, :, low:high], both(1, 0), both(1, 1),
        )
        for tile, pair in tiles.add(head, mask, output, output_dot):
            for t in (0, 1):
                attended[t * places:(t + 1) * places, tile * LANES:(tile + 1) * LANES] = pair[t].astype(jnp.bfloat16)
        serve(head + 1)

    serve_all(0)
    all_here(0)
    own_copies[0].wait()

    @pl.loop(0, width // TILE)
    def _(index):
        columns = pl.ds(pl.multiple_of(index * TILE, TILE), TILE)
        projected = across(attended[...], out_all[columns, :])
        gate, gate_slope = mod[0:1, columns], mod[3:4, columns]
        residual[0, 0, :, columns] = stream[0, 0, :, columns].astype(jnp.float32) + gate * projected[:places]
        residual[1, 0, :, columns] = (
            stream[1, 0, :, columns].astype(jnp.float32)
            + gate_slope * projected[:places]
            + gate * projected[places:]
        )

    serve(18)
    row_copies = []
    for k in list(range(1, n)) + [0]:
        frame = lax.rem(me + k, n)
        rows = pl.ds(pl.multiple_of(frame * part, 8), part)
        hidden, hidden_dot = residual[0, 0, rows, :], residual[1, 0, rows, :]
        centered = hidden - jnp.mean(hidden, axis=-1, keepdims=True)
        inv_scale = lax.rsqrt(jnp.mean(centered * centered, axis=-1, keepdims=True) + 1e-06)
        normed = centered * inv_scale
        normed_dot = (
            hidden_dot
            - jnp.mean(hidden_dot, axis=-1, keepdims=True)
            - normed * jnp.mean(normed * hidden_dot, axis=-1, keepdims=True)
        ) * inv_scale
        modulated = normed * (1.0 + mod[2:3, :]) + mod[1:2, :]
        modulated_dot = normed_dot * (1.0 + mod[2:3, :]) + normed * mod[5:6, :] + mod[4:5, :]
        block = jnp.concatenate([modulated, modulated_dot], axis=0).astype(jnp.bfloat16)
        mine = pl.ds(pl.multiple_of(me * 2 * part, 16), 2 * part)
        if k == 0:
            rows_recv[mine, :] = block
        else:
            theirs = pl.ds(pl.multiple_of(frame * 2 * part, 16), 2 * part)
            rows_send[theirs, :] = block
            row_copies.append(remote(
                rows_send.at[theirs], rows_recv.at[mine], row_send_sem.at[k], row_recv_sem.at[k], {"frame": frame}
            ))
            row_copies[-1].start()

    serve_all(1)
    all_here(1)
    own_copies[1].wait()
    for k in range(1, n):
        source = lax.rem(me - k + n, n)
        arrives(rows_recv.at[pl.ds(pl.multiple_of(source * 2 * part, 16), 2 * part)], row_recv_sem.at[k]).wait_recv()

    @pl.loop(0, 3 * width // TILE)
    def _(index):
        columns = pl.ds(pl.multiple_of(index * TILE, TILE), TILE)
        product = across(rows_recv[...], qkv_all[columns, :])
        for t in (0, 1):
            kept = [product[(2 * f + t) * part:(2 * f + t + 1) * part] for f in range(n)]
            qkv[t, :, columns] = jnp.concatenate(kept, axis=0).astype(jnp.bfloat16)

    rows = n * part
    one = lax.rem(lax.broadcasted_iota(jnp.int32, (rows, rows), 0), part)
    two = lax.rem(lax.broadcasted_iota(jnp.int32, (rows, rows), 1), part)
    allowed = one == two
    tiles = LaneTiles(heads)
    chunks = back_send.shape[0]
    chunk_tiles = width // LANES // chunks
    back_copies = []
    pieces = {}
    for head in range(heads):
        low, high = lane_window(head)
        mask = head_mask(head, low, high)
        take = lambda t, j: qkv[t, :, j * width + low:j * width + high]
        output, output_dot = attend_head(
            mask, take(0, 0), take(0, 1), take(0, 2), take(1, 0), take(1, 1), take(1, 2), allowed
        )
        for tile, pair in tiles.add(head, mask, output, output_dot):
            chunk, inner = tile // chunk_tiles, tile % chunk_tiles
            for f in range(n):
                block = jnp.concatenate([value[f * part:(f + 1) * part] for value in pair], axis=0)
                back_send[chunk, f, :, inner * LANES:(inner + 1) * LANES] = block.astype(jnp.bfloat16)
            if inner == chunk_tiles - 1:
                own = pltpu.make_async_copy(
                    back_send.at[chunk, me], returned.at[chunk, me], back_send_sem.at[chunk, 0]
                )
                own.start()
                back_copies.append(own)
                for k in range(1, n):
                    frame = lax.rem(me + k, n)
                    copy = remote(
                        back_send.at[chunk, frame], returned.at[chunk, me],
                        back_send_sem.at[chunk, k], back_recv_sem.at[chunk, k], {"frame": frame},
                    )
                    copy.start()
                    pieces[chunk, k] = copy

    kv_copy.wait_send()
    for which in (0, 1):
        for step in range(1, n):
            ring_copy(which, step).wait_send()
            core_copy(which, step).wait_send()

            @pl.when(core == 0)
            def _():
                x_copy(which, step).wait_send()
                xcore_copy(which, step).wait_send()

    for copy in row_copies:
        copy.wait_send()
    for copy in back_copies:
        copy.wait()
    for (chunk, k), copy in pieces.items():
        copy.wait_send()
        source = lax.rem(me - k + n, n)
        arrives(returned.at[chunk, source], back_recv_sem.at[chunk, k]).wait_recv()


def per_device_fused(n, stream, spatial_qkv, out_weight, qkv_weight, mod_table, timestep):
    places, width = stream.shape[2], stream.shape[3]
    part = places // n
    chunks = width // TILE
    mod = jnp.concatenate(modulation(mod_table, timestep), axis=0)
    bf16, f32 = jnp.bfloat16, jnp.float32
    dma = pltpu.SemaphoreType.DMA
    vmem = pl.BlockSpec(memory_space=pltpu.VMEM)
    residual, returned = pl.pallas_call(
        functools.partial(fused_kernel, n),
        out_shape=(
            jax.ShapeDtypeStruct(stream.shape, f32),
            jax.ShapeDtypeStruct((chunks, n, 2 * part, TILE), bf16),
        ),
        in_specs=[vmem] * 5,
        out_specs=(vmem, vmem),
        scratch_shapes=[
            pltpu.VMEM((2, 2, places, width), bf16),
            pltpu.VMEM((width, width), bf16),
            pltpu.VMEM((3 * width, width), bf16),
            pltpu.VMEM((2 * places, width), bf16),
            pltpu.VMEM((2 * places, width), bf16),
            pltpu.VMEM((2 * places, width), bf16),
            pltpu.VMEM((2, places, 3 * width), bf16),
            pltpu.VMEM((chunks, n, 2 * part, TILE), bf16),
            dma((2,)), dma((2,)),
        ] + [dma((2, n))] * 8 + [dma((n,))] * 2 + [dma((chunks, n))] * 2,
        compiler_params=pltpu.CompilerParams(
            collective_id=0, has_side_effects=True, vmem_limit_bytes=56 * 1024 * 1024
        ),
    )(spatial_qkv, stream, out_weight.T, qkv_weight.T, mod)
    temporal = returned.reshape(chunks, n, 2, part, TILE)
    temporal = jnp.transpose(temporal, (2, 1, 3, 0, 4)).reshape(stream.shape).astype(f32)
    return (residual, temporal)


def fits_fused(mesh, places, width, out_columns, qkv_columns, frames_local):
    n = mesh.shape["frame"]
    return (
        mesh.shape["pix"] == 2
        and mesh.shape["clips"] % 2 == 0
        and n % 2 == 0
        and frames_local == 1
        and places % n == 0
        and (places // n) % 8 == 0
        and places % 16 == 0
        and width % TILE == 0
        and width % HEAD_DIM == 0
        and out_columns % 48 == 0
        and qkv_columns % 48 == 0
    )


def solution(mesh):
    in_specs = (
        P(None, ("clips", "frame"), "pix", None),
        P(None, None, ("clips", "frame"), "pix", None),
        P(None, "frame"),
        P(None, "frame"),
        P(),
        P("clips"),
    )
    out_specs = (P(None, ("clips", "frame"), "pix", None), P(None, ("clips", "frame"), "pix", None))

    def local(stream, spatial_qkv, out_weight, qkv_weight, mod_table, timestep):
        args = (stream, spatial_qkv, out_weight, qkv_weight, mod_table, timestep)
        if fits_fused(
            mesh, stream.shape[2], stream.shape[3], out_weight.shape[1], qkv_weight.shape[1], stream.shape[1]
        ):
            return per_device_fused(mesh.shape["frame"], *args)
        return per_device(*args)

    return jax.shard_map(local, mesh=mesh, in_specs=in_specs, out_specs=out_specs, check_vma=False)
```

```python
import functools
import math

import jax
import jax.numpy as jnp
from jax import lax
from jax.experimental import pallas as pl
from jax.experimental.pallas import tpu as pltpu
from jax.sharding import PartitionSpec as P

HEAD_DIM = 72
LANES = 128
TILE = 384


def modulation(mod_table, timestep):
    width = mod_table.shape[-1]
    frequency = jnp.exp(-math.log(10.0) * jnp.arange(width).astype(jnp.float32) / width)
    time_value = timestep[0].astype(jnp.float32) * (math.pi / 1000.0)
    mod_value = mod_table[:, 0] + mod_table[:, 1] * jnp.cos(frequency * time_value)
    mod_slope = -mod_table[:, 1] * frequency * jnp.sin(frequency * time_value)
    return (mod_value, mod_slope)


def attend_group(inputs):
    query, keys, values, query_dot, keys_dot, values_dot = inputs
    scale = 1.0 / math.sqrt(query.shape[-1])
    scores = jnp.einsum("blhe,bmhe->bhlm", query, keys, preferred_element_type=jnp.float32) * scale
    scores_dot = (
        jnp.einsum("blhe,bmhe->bhlm", query_dot, keys, preferred_element_type=jnp.float32)
        + jnp.einsum("blhe,bmhe->bhlm", query, keys_dot, preferred_element_type=jnp.float32)
    ) * scale
    top_score = jnp.max(scores, axis=-1, keepdims=True)
    expo = jnp.exp(scores - top_score)
    probs = expo / jnp.sum(expo, axis=-1, keepdims=True)
    probs_low = probs.astype(jnp.bfloat16)
    output = jnp.einsum("bhlm,bmhe->blhe", probs_low, values, preferred_element_type=jnp.float32)
    row_total = jnp.sum(probs * scores_dot, axis=-1, keepdims=True)
    weighted = probs * (scores_dot - row_total)
    weighted_low = weighted.astype(jnp.bfloat16)
    output_dot = jnp.einsum(
        "bhlm,bmhe->blhe", weighted_low, values, preferred_element_type=jnp.float32
    ) + jnp.einsum("bhlm,bmhe->blhe", probs_low, values_dot, preferred_element_type=jnp.float32)
    return (output, output_dot)


def attend(stacked, group_size):
    batch, length, heads_all, head_size = stacked.shape[2:]
    groups = heads_all // group_size
    shaped = stacked.reshape(2, 3, batch, length, groups, group_size, head_size)
    shaped = jnp.transpose(shaped, (4, 0, 1, 2, 3, 5, 6))
    inputs = (
        shaped[:, 0, 0],
        shaped[:, 0, 1],
        shaped[:, 0, 2],
        shaped[:, 1, 0],
        shaped[:, 1, 1],
        shaped[:, 1, 2],
    )
    output, output_dot = lax.map(attend_group, inputs)
    joined = jnp.stack([output, output_dot], axis=1)
    joined = jnp.transpose(joined, (1, 2, 3, 0, 4, 5))
    return joined.reshape(2, batch, length, heads_all * head_size)


def per_device(stream, spatial_qkv, out_weight, qkv_weight, mod_table, timestep):
    frames_local = stream.shape[1]
    places = stream.shape[2]
    width = stream.shape[3]
    block = lax.all_to_all(spatial_qkv, "pix", split_axis=4, concat_axis=3, tiled=True)
    frames_here = block.shape[2]
    length = block.shape[3]
    channels = block.shape[4]
    shaped = block.reshape(2, 3, frames_here, length, channels // HEAD_DIM, HEAD_DIM)
    attended = attend(shaped, 1).astype(jnp.bfloat16)
    spatial = lax.all_to_all(attended, "pix", split_axis=2, concat_axis=3, tiled=True)
    flat_spatial = spatial.reshape(-1, width)
    projected = jnp.dot(
        flat_spatial,
        lax.all_gather(out_weight, "frame", axis=1, tiled=True),
        preferred_element_type=jnp.float32,
    )
    projected = projected.reshape(2, frames_local, places, width)
    mod_value, mod_slope = modulation(mod_table, timestep)
    primal_in = stream[0].astype(jnp.float32)
    tangent_in = stream[1].astype(jnp.float32)
    hidden = primal_in + mod_value[0] * projected[0]
    hidden_dot = tangent_in + mod_slope[0] * projected[0] + mod_value[0] * projected[1]
    centered = hidden - jnp.mean(hidden, axis=-1, keepdims=True)
    inv_scale = lax.rsqrt(jnp.mean(centered * centered, axis=-1, keepdims=True) + 1e-06)
    normed = centered * inv_scale
    normed_dot = (
        hidden_dot
        - jnp.mean(hidden_dot, axis=-1, keepdims=True)
        - normed * jnp.mean(normed * hidden_dot, axis=-1, keepdims=True)
    ) * inv_scale
    modulated = normed * (1.0 + mod_value[2]) + mod_value[1]
    modulated_dot = normed_dot * (1.0 + mod_value[2]) + normed * mod_slope[2] + mod_slope[1]
    modulated_low = jnp.stack([modulated, modulated_dot]).astype(jnp.bfloat16)
    moved_rows = lax.all_to_all(modulated_low, "frame", split_axis=2, concat_axis=1, tiled=True)
    frames_all = moved_rows.shape[1]
    sub_places = moved_rows.shape[2]
    flat_rows = moved_rows.reshape(-1, width)
    projected_qkv = (
        jnp.dot(
            flat_rows,
            lax.all_gather(qkv_weight, "frame", axis=1, tiled=True),
            preferred_element_type=jnp.float32,
        )
        .astype(jnp.bfloat16)
        .reshape(2, frames_all, sub_places, 3, width)
    )
    moved = jnp.transpose(projected_qkv, (0, 3, 1, 2, 4))
    frames_all = moved.shape[2]
    sub_places = moved.shape[3]
    arranged = jnp.transpose(moved, (0, 1, 3, 2, 4)).reshape(
        2, 3, sub_places, frames_all, width // HEAD_DIM, HEAD_DIM
    )
    attended = attend(arranged, width // HEAD_DIM)
    attended = jnp.transpose(attended, (0, 2, 1, 3))
    temporal = lax.all_to_all(attended, "frame", split_axis=1, concat_axis=2, tiled=True)
    residual = jnp.stack([hidden, hidden_dot])
    return (residual, temporal)


def lane_window(head):
    low = head * HEAD_DIM // LANES * LANES
    high = -(-(head * HEAD_DIM + HEAD_DIM) // LANES) * LANES
    return low, high


def head_mask(head, low, high):
    lane = lax.broadcasted_iota(jnp.int32, (1, high - low), 1) + low
    return (lane >= head * HEAD_DIM) & (lane < (head + 1) * HEAD_DIM)


def across(left, right):
    return lax.dot_general(left, right, (((1,), (1,)), ((), ())), preferred_element_type=jnp.float32)


def attend_head(mask, query, keys, values, query_dot, keys_dot, values_dot, allowed=None):
    scale = 1.0 / math.sqrt(HEAD_DIM)
    keep = mask.astype(jnp.float32).astype(jnp.bfloat16)
    rows = query.shape[0]
    query = query * keep
    query_dot = query_dot * keep
    both = across(jnp.concatenate([query, query_dot], axis=0), keys)
    scores = both[:rows] * scale
    scores_dot = (both[rows:] + across(query, keys_dot)) * scale
    if allowed is not None:
        scores = jnp.where(allowed, scores, -jnp.inf)
    expo = jnp.exp(scores - jnp.max(scores, axis=-1, keepdims=True))
    probs = expo * (1.0 / jnp.sum(expo, axis=-1, keepdims=True))
    weighted = probs * (scores_dot - jnp.sum(probs * scores_dot, axis=-1, keepdims=True))
    probs_low = probs.astype(jnp.bfloat16)
    stacked = jnp.concatenate([probs_low, weighted.astype(jnp.bfloat16)], axis=0)
    both = jnp.dot(stacked, values, preferred_element_type=jnp.float32)
    output_dot = both[rows:] + jnp.dot(probs_low, values_dot, preferred_element_type=jnp.float32)
    return both[:rows], output_dot


class LaneTiles:
    def __init__(self, heads):
        self.held = {}
        self.last = {}
        for head in range(heads):
            low, high = lane_window(head)
            for tile in range(low // LANES, high // LANES):
                self.last[tile] = head

    def add(self, head, mask, output, output_dot):
        low, high = lane_window(head)
        done = []
        for tile in range(low // LANES, high // LANES):
            part = slice(tile * LANES - low, (tile + 1) * LANES - low)
            here = mask[:, part]
            pair = (output[:, part], output_dot[:, part])
            if tile in self.held:
                pair = tuple(jnp.where(here, a, b) for a, b in zip(pair, self.held[tile]))
            self.held[tile] = pair
            if self.last[tile] == head:
                done.append((tile, self.held.pop(tile)))
        return done


def fused_kernel(
    n, spatial, stream, out_own, qkv_own, mod, residual, returned,
    peer_kv, out_all, qkv_all, attended, rows_send, rows_recv, qkv, back_send,
    kv_sem, own_sem, up_send, down_send, row_send, grid_recv, core_send, core_recv, x_send, x_recv,
    xcore_send, xcore_recv, row_send_sem, row_recv_sem, back_send_sem, back_recv_sem,
):
    clip, core, me = lax.axis_index("clips"), lax.axis_index("pix"), lax.axis_index("frame")
    side = lax.rem(clip, 2)
    x_peer = clip + 1 - 2 * side
    places, width = stream.shape[2], stream.shape[3]
    part = places // n
    heads = width // HEAD_DIM
    half = n // 2

    depth, row = lax.div(me, 2), lax.rem(me, 2)
    depths = n // 2
    to_peer = {"pix": 1 - core}
    to_x = {"clips": x_peer}
    to_row = {"frame": 2 * depth + 1 - row}

    barrier = pltpu.get_barrier_semaphore()
    for target in [to_peer, to_x] + [{"frame": lax.rem(me + k, n)} for k in range(1, n)]:
        pl.semaphore_signal(barrier, inc=1, device_id=target, device_id_type=pl.DeviceIdType.MESH)
    pl.semaphore_wait(barrier, n + 1)

    def remote(source, target, send, recv, device):
        return pltpu.make_async_remote_copy(
            src_ref=source, dst_ref=target, send_sem=send, recv_sem=recv,
            device_id=device, device_id_type=pl.DeviceIdType.MESH,
        )

    kv_copy = remote(spatial.at[:, 1:3, 0], peer_kv, kv_sem.at[0], kv_sem.at[1], to_peer)
    kv_copy.start()

    gathered = (out_all, qkv_all)
    owned = (out_own, qkv_own)
    sizes = tuple(ref.shape[0] for ref in owned)
    my_third = core + (1 - core) * 2 * side
    peer_third = (1 - core) + core * 2 * side
    x_third = 2 * (1 - side)

    def piece(which, frame, third):
        size = sizes[which] // 3
        return gathered[which].at[pl.ds(pl.multiple_of(frame * sizes[which] + third * size, 16), size)]

    def arrives(block, recv):
        return remote(block, block, kv_sem.at[0], recv, to_peer)

    def moves(which, frame, third, send, recv, device):
        block = piece(which, frame, third)
        return remote(block, block, send.at[which, frame], recv.at[which, frame], device)

    def own_move(which, send, device):
        size = sizes[which] // 3
        source = owned[which].at[pl.ds(pl.multiple_of(my_third * size, 16), size)]
        return remote(
            source, piece(which, me, my_third), send.at[which, me], grid_recv.at[which, me], device
        )

    line_copy = lambda which, frame, sign: moves(
        which, frame, my_third, up_send if sign > 0 else down_send, grid_recv, {"frame": me + 2 * sign}
    )
    row_copy = lambda which, frame: moves(which, frame, my_third, row_send, grid_recv, to_row)
    core_copy = lambda which, frame: moves(which, frame, my_third, core_send, core_recv, to_peer)
    x_copy = lambda which, frame: moves(which, frame, my_third, x_send, x_recv, to_x)
    xcore_copy = lambda which, frame: moves(which, frame, x_third, xcore_send, xcore_recv, to_peer)

    def inside(offset):
        return (depth + offset >= 0) & (depth + offset < depths)

    def when_core(which_core, act):
        pl.when(core == which_core)(act)

    def line_step(which, distance):
        for sign in (1, -1):
            @pl.when(inside(-sign * distance))
            def _():
                frame = me - 2 * sign * distance
                arrives(piece(which, frame, my_third), grid_recv.at[which, frame]).wait_recv()

                @pl.when(inside(sign))
                def _():
                    line_copy(which, frame, sign).start()

                row_copy(which, frame).start()
                when_core(0, lambda: x_copy(which, frame).start())
                core_copy(which, frame).start()

    def offsets(distance):
        return (1, -1) if distance else (1,)

    def row_step(which, distance):
        for sign in offsets(distance):
            @pl.when(inside(sign * distance))
            def _():
                frame = 2 * (depth + sign * distance) + 1 - row
                arrives(piece(which, frame, my_third), grid_recv.at[which, frame]).wait_recv()
                when_core(0, lambda: x_copy(which, frame).start())
                core_copy(which, frame).start()

    def x_step(which, distance, turn):
        for sign in offsets(distance):
            @pl.when(inside(sign * distance) & (core == 0))
            def _():
                frame = 2 * (depth + sign * distance) + (1 - turn) * row + turn * (1 - row)
                arrives(piece(which, frame, x_third), x_recv.at[which, frame]).wait_recv()
                xcore_copy(which, frame).start()

    def all_here(which):
        for k in range(1, n):
            frame = lax.rem(me + k, n)
            arrives(piece(which, frame, peer_third), core_recv.at[which, frame]).wait_recv()
            when_core(
                1, lambda: arrives(piece(which, frame, x_third), xcore_recv.at[which, frame]).wait_recv()
            )

    def all_sent(which):
        own_move(which, row_send, to_row).wait_send()
        for sign in (1, -1):
            @pl.when(inside(sign))
            def _():
                own_move(which, up_send if sign > 0 else down_send, {"frame": me + 2 * sign}).wait_send()

            for distance in range(1, depths):
                @pl.when(inside(-sign * distance))
                def _():
                    frame = me - 2 * sign * distance
                    row_copy(which, frame).wait_send()

                    @pl.when(inside(sign))
                    def _():
                        line_copy(which, frame, sign).wait_send()

        for k in range(1, n):
            frame = lax.rem(me + k, n)
            core_copy(which, frame).wait_send()

            @pl.when(core == 0)
            def _():
                x_copy(which, frame).wait_send()
                xcore_copy(which, frame).wait_send()

    own_copies = []
    for which in (0, 1):
        for sign in (1, -1):
            @pl.when(inside(sign))
            def _():
                own_move(which, up_send if sign > 0 else down_send, {"frame": me + 2 * sign}).start()

        own_move(which, row_send, to_row).start()
        whole = gathered[which].at[pl.ds(pl.multiple_of(me * sizes[which], 16), sizes[which])]
        own_copies.append(pltpu.make_async_copy(owned[which], whole, own_sem.at[which]))
        own_copies[-1].start()

    events = []
    for distance in range(depths):
        if distance:
            events.append((2 * distance, line_step, (0, distance)))
            events.append((4 * distance + 1, line_step, (1, distance)))
            events.append((2 * distance + 3, x_step, (0, distance, 0)))
            events.append((4 * distance + 6, x_step, (1, distance, 0)))
        events.append((2 * distance + 2.5, row_step, (0, distance)))
        events.append((4 * distance + 5, row_step, (1, distance)))
        events.append((2 * distance + 5, x_step, (0, distance, 1)))
        events.append((4 * distance + 8, x_step, (1, distance, 1)))
    events.sort(key=lambda event: event[0])

    def serve(until):
        while events and events[0][0] <= until:
            _, act, args = events.pop(0)
            act(*args)

    def serve_all(which):
        for event in [event for event in events if event[2][0] == which]:
            events.remove(event)
            event[1](*event[2])

    kv_copy.wait_recv()
    tiles = LaneTiles(heads)
    for head in range(heads):
        low, high = lane_window(head)
        mask = head_mask(head, low, high)
        both = lambda t, j: jnp.concatenate([spatial[t, 1 + j, 0, :, low:high], peer_kv[t, j, :, low:high]], axis=0)
        output, output_dot = attend_head(
            mask, spatial[0, 0, 0, :, low:high], both(0, 0), both(0, 1),
            spatial[1, 0, 0, :, low:high], both(1, 0), both(1, 1),
        )
        for tile, pair in tiles.add(head, mask, output, output_dot):
            for t in (0, 1):
                attended[t * places:(t + 1) * places, tile * LANES:(tile + 1) * LANES] = pair[t].astype(jnp.bfloat16)
        serve(head + 1)

    serve_all(0)
    all_here(0)
    own_copies[0].wait()

    @pl.loop(0, width // TILE)
    def _(index):
        columns = pl.ds(pl.multiple_of(index * TILE, TILE), TILE)
        projected = across(attended[...], out_all[columns, :])
        gate, gate_slope = mod[0:1, columns], mod[3:4, columns]
        residual[0, 0, :, columns] = stream[0, 0, :, columns].astype(jnp.float32) + gate * projected[:places]
        residual[1, 0, :, columns] = (
            stream[1, 0, :, columns].astype(jnp.float32)
            + gate_slope * projected[:places]
            + gate * projected[places:]
        )

    serve(17)
    row_copies = []
    for k in list(range(1, n)) + [0]:
        frame = lax.rem(me + k, n)
        rows = pl.ds(pl.multiple_of(frame * part, 8), part)
        hidden, hidden_dot = residual[0, 0, rows, :], residual[1, 0, rows, :]
        centered = hidden - jnp.mean(hidden, axis=-1, keepdims=True)
        inv_scale = lax.rsqrt(jnp.mean(centered * centered, axis=-1, keepdims=True) + 1e-06)
        normed = centered * inv_scale
        normed_dot = (
            hidden_dot
            - jnp.mean(hidden_dot, axis=-1, keepdims=True)
            - normed * jnp.mean(normed * hidden_dot, axis=-1, keepdims=True)
        ) * inv_scale
        modulated = normed * (1.0 + mod[2:3, :]) + mod[1:2, :]
        modulated_dot = normed_dot * (1.0 + mod[2:3, :]) + normed * mod[5:6, :] + mod[4:5, :]
        block = jnp.concatenate([modulated, modulated_dot], axis=0).astype(jnp.bfloat16)
        mine = pl.ds(pl.multiple_of(me * 2 * part, 16), 2 * part)
        if k == 0:
            rows_recv[mine, :] = block
        else:
            theirs = pl.ds(pl.multiple_of(frame * 2 * part, 16), 2 * part)
            rows_send[theirs, :] = block
            row_copies.append(remote(
                rows_send.at[theirs], rows_recv.at[mine], row_send_sem.at[k], row_recv_sem.at[k], {"frame": frame}
            ))
            row_copies[-1].start()
        serve(18 + k)

    serve_all(1)
    all_here(1)
    own_copies[1].wait()
    for k in range(1, n):
        source = lax.rem(me - k + n, n)
        arrives(rows_recv.at[pl.ds(pl.multiple_of(source * 2 * part, 16), 2 * part)], row_recv_sem.at[k]).wait_recv()

    def project_chunk(chunk):
        @pl.loop(0, 3)
        def _(index):
            columns = pl.ds(pl.multiple_of(index * width + chunk * TILE, LANES), TILE)
            product = across(rows_recv[...], qkv_all[columns, :])
            for t in (0, 1):
                kept = [product[(2 * f + t) * part:(2 * f + t + 1) * part] for f in range(n)]
                qkv[t, :, columns] = jnp.concatenate(kept, axis=0).astype(jnp.bfloat16)

    rows = n * part
    one = lax.rem(lax.broadcasted_iota(jnp.int32, (rows, rows), 0), part)
    two = lax.rem(lax.broadcasted_iota(jnp.int32, (rows, rows), 1), part)
    allowed = one == two
    tiles = LaneTiles(heads)
    chunks = back_send.shape[0]
    chunk_tiles = width // LANES // chunks
    back_copies = []
    pieces = {}
    ready = 0
    for head in range(heads):
        low, high = lane_window(head)
        while ready * TILE < high:
            project_chunk(ready)
            ready += 1
        mask = head_mask(head, low, high)
        take = lambda t, j: qkv[t, :, j * width + low:j * width + high]
        output, output_dot = attend_head(
            mask, take(0, 0), take(0, 1), take(0, 2), take(1, 0), take(1, 1), take(1, 2), allowed
        )
        for tile, pair in tiles.add(head, mask, output, output_dot):
            chunk, inner = tile // chunk_tiles, tile % chunk_tiles
            for f in range(n):
                block = jnp.concatenate([value[f * part:(f + 1) * part] for value in pair], axis=0)
                back_send[chunk, f, :, inner * LANES:(inner + 1) * LANES] = block.astype(jnp.bfloat16)
            if inner == chunk_tiles - 1:
                own = pltpu.make_async_copy(
                    back_send.at[chunk, me], returned.at[chunk, me], back_send_sem.at[chunk, 0]
                )
                own.start()
                back_copies.append(own)
                for k in range(1, n):
                    frame = lax.rem(me + k, n)
                    copy = remote(
                        back_send.at[chunk, frame], returned.at[chunk, me],
                        back_send_sem.at[chunk, k], back_recv_sem.at[chunk, k], {"frame": frame},
                    )
                    copy.start()
                    pieces[chunk, k] = copy

    kv_copy.wait_send()
    for which in (0, 1):
        all_sent(which)
    for copy in row_copies:
        copy.wait_send()
    for copy in back_copies:
        copy.wait()
    for (chunk, k), copy in pieces.items():
        copy.wait_send()
        source = lax.rem(me - k + n, n)
        arrives(returned.at[chunk, source], back_recv_sem.at[chunk, k]).wait_recv()


def finish_kernel(residual, returned, residual_out, temporal, sem):
    copy = pltpu.make_async_copy(residual, residual_out, sem)
    copy.start()
    chunks, n, rows, tile = returned.shape
    part = rows // 2
    for chunk in range(chunks):
        for f in range(n):
            block = returned[chunk, f].astype(jnp.float32)
            for t in (0, 1):
                temporal[t, 0, f * part:(f + 1) * part, chunk * tile:(chunk + 1) * tile] = (
                    block[t * part:(t + 1) * part]
                )
    copy.wait()


def per_device_fused(n, stream, spatial_qkv, out_weight, qkv_weight, mod_table, timestep):
    places, width = stream.shape[2], stream.shape[3]
    part = places // n
    chunks = width // TILE
    mod = jnp.concatenate(modulation(mod_table, timestep), axis=0)
    bf16, f32 = jnp.bfloat16, jnp.float32
    dma = pltpu.SemaphoreType.DMA
    vmem = pl.BlockSpec(memory_space=pltpu.VMEM)
    residual, returned = pl.pallas_call(
        functools.partial(fused_kernel, n),
        out_shape=(
            jax.ShapeDtypeStruct(stream.shape, f32),
            jax.ShapeDtypeStruct((chunks, n, 2 * part, TILE), bf16),
        ),
        in_specs=[vmem] * 5,
        out_specs=(vmem, vmem),
        scratch_shapes=[
            pltpu.VMEM((2, 2, places, width), bf16),
            pltpu.VMEM((width, width), bf16),
            pltpu.VMEM((3 * width, width), bf16),
            pltpu.VMEM((2 * places, width), bf16),
            pltpu.VMEM((2 * places, width), bf16),
            pltpu.VMEM((2 * places, width), bf16),
            pltpu.VMEM((2, places, 3 * width), bf16),
            pltpu.VMEM((chunks, n, 2 * part, TILE), bf16),
            dma((2,)), dma((2,)),
        ] + [dma((2, n))] * 10 + [dma((n,))] * 2 + [dma((chunks, n))] * 2,
        compiler_params=pltpu.CompilerParams(
            collective_id=0, has_side_effects=True, vmem_limit_bytes=56 * 1024 * 1024
        ),
    )(spatial_qkv, stream, out_weight.T, qkv_weight.T, mod)
    return tuple(pl.pallas_call(
        finish_kernel,
        out_shape=(jax.ShapeDtypeStruct(stream.shape, f32),) * 2,
        in_specs=[pl.BlockSpec(memory_space=pl.ANY), vmem],
        out_specs=(pl.BlockSpec(memory_space=pl.ANY), vmem),
        scratch_shapes=[dma],
        compiler_params=pltpu.CompilerParams(vmem_limit_bytes=32 * 1024 * 1024),
    )(residual, returned))


def fits_fused(mesh, places, width, out_columns, qkv_columns, frames_local):
    n = mesh.shape["frame"]
    return (
        mesh.shape["pix"] == 2
        and mesh.shape["clips"] % 2 == 0
        and n % 2 == 0
        and frames_local == 1
        and places % n == 0
        and (places // n) % 8 == 0
        and places % 16 == 0
        and width % TILE == 0
        and width % HEAD_DIM == 0
        and out_columns % 48 == 0
        and qkv_columns % 48 == 0
    )


def solution(mesh):
    in_specs = (
        P(None, ("clips", "frame"), "pix", None),
        P(None, None, ("clips", "frame"), "pix", None),
        P(None, "frame"),
        P(None, "frame"),
        P(),
        P("clips"),
    )
    out_specs = (P(None, ("clips", "frame"), "pix", None), P(None, ("clips", "frame"), "pix", None))

    def local(stream, spatial_qkv, out_weight, qkv_weight, mod_table, timestep):
        args = (stream, spatial_qkv, out_weight, qkv_weight, mod_table, timestep)
        if fits_fused(
            mesh, stream.shape[2], stream.shape[3], out_weight.shape[1], qkv_weight.shape[1], stream.shape[1]
        ):
            return per_device_fused(mesh.shape["frame"], *args)
        return per_device(*args)

    return jax.shard_map(local, mesh=mesh, in_specs=in_specs, out_specs=out_specs, check_vma=False)
```

```python
import functools
import math

import jax
import jax.numpy as jnp
from jax import lax
from jax.experimental import pallas as pl
from jax.experimental.pallas import tpu as pltpu
from jax.sharding import PartitionSpec as P

HEAD_DIM = 72
LANES = 128
TILE = 384


def modulation(mod_table, timestep):
    width = mod_table.shape[-1]
    frequency = jnp.exp(-math.log(10.0) * jnp.arange(width).astype(jnp.float32) / width)
    time_value = timestep[0].astype(jnp.float32) * (math.pi / 1000.0)
    mod_value = mod_table[:, 0] + mod_table[:, 1] * jnp.cos(frequency * time_value)
    mod_slope = -mod_table[:, 1] * frequency * jnp.sin(frequency * time_value)
    return (mod_value, mod_slope)


def attend_group(inputs):
    query, keys, values, query_dot, keys_dot, values_dot = inputs
    scale = 1.0 / math.sqrt(query.shape[-1])
    scores = jnp.einsum("blhe,bmhe->bhlm", query, keys, preferred_element_type=jnp.float32) * scale
    scores_dot = (
        jnp.einsum("blhe,bmhe->bhlm", query_dot, keys, preferred_element_type=jnp.float32)
        + jnp.einsum("blhe,bmhe->bhlm", query, keys_dot, preferred_element_type=jnp.float32)
    ) * scale
    top_score = jnp.max(scores, axis=-1, keepdims=True)
    expo = jnp.exp(scores - top_score)
    probs = expo / jnp.sum(expo, axis=-1, keepdims=True)
    probs_low = probs.astype(jnp.bfloat16)
    output = jnp.einsum("bhlm,bmhe->blhe", probs_low, values, preferred_element_type=jnp.float32)
    row_total = jnp.sum(probs * scores_dot, axis=-1, keepdims=True)
    weighted = probs * (scores_dot - row_total)
    weighted_low = weighted.astype(jnp.bfloat16)
    output_dot = jnp.einsum(
        "bhlm,bmhe->blhe", weighted_low, values, preferred_element_type=jnp.float32
    ) + jnp.einsum("bhlm,bmhe->blhe", probs_low, values_dot, preferred_element_type=jnp.float32)
    return (output, output_dot)


def attend(stacked, group_size):
    batch, length, heads_all, head_size = stacked.shape[2:]
    groups = heads_all // group_size
    shaped = stacked.reshape(2, 3, batch, length, groups, group_size, head_size)
    shaped = jnp.transpose(shaped, (4, 0, 1, 2, 3, 5, 6))
    inputs = (
        shaped[:, 0, 0],
        shaped[:, 0, 1],
        shaped[:, 0, 2],
        shaped[:, 1, 0],
        shaped[:, 1, 1],
        shaped[:, 1, 2],
    )
    output, output_dot = lax.map(attend_group, inputs)
    joined = jnp.stack([output, output_dot], axis=1)
    joined = jnp.transpose(joined, (1, 2, 3, 0, 4, 5))
    return joined.reshape(2, batch, length, heads_all * head_size)


def per_device(stream, spatial_qkv, out_weight, qkv_weight, mod_table, timestep):
    frames_local = stream.shape[1]
    places = stream.shape[2]
    width = stream.shape[3]
    block = lax.all_to_all(spatial_qkv, "pix", split_axis=4, concat_axis=3, tiled=True)
    frames_here = block.shape[2]
    length = block.shape[3]
    channels = block.shape[4]
    shaped = block.reshape(2, 3, frames_here, length, channels // HEAD_DIM, HEAD_DIM)
    attended = attend(shaped, 1).astype(jnp.bfloat16)
    spatial = lax.all_to_all(attended, "pix", split_axis=2, concat_axis=3, tiled=True)
    flat_spatial = spatial.reshape(-1, width)
    projected = jnp.dot(
        flat_spatial,
        lax.all_gather(out_weight, "frame", axis=1, tiled=True),
        preferred_element_type=jnp.float32,
    )
    projected = projected.reshape(2, frames_local, places, width)
    mod_value, mod_slope = modulation(mod_table, timestep)
    primal_in = stream[0].astype(jnp.float32)
    tangent_in = stream[1].astype(jnp.float32)
    hidden = primal_in + mod_value[0] * projected[0]
    hidden_dot = tangent_in + mod_slope[0] * projected[0] + mod_value[0] * projected[1]
    centered = hidden - jnp.mean(hidden, axis=-1, keepdims=True)
    inv_scale = lax.rsqrt(jnp.mean(centered * centered, axis=-1, keepdims=True) + 1e-06)
    normed = centered * inv_scale
    normed_dot = (
        hidden_dot
        - jnp.mean(hidden_dot, axis=-1, keepdims=True)
        - normed * jnp.mean(normed * hidden_dot, axis=-1, keepdims=True)
    ) * inv_scale
    modulated = normed * (1.0 + mod_value[2]) + mod_value[1]
    modulated_dot = normed_dot * (1.0 + mod_value[2]) + normed * mod_slope[2] + mod_slope[1]
    modulated_low = jnp.stack([modulated, modulated_dot]).astype(jnp.bfloat16)
    moved_rows = lax.all_to_all(modulated_low, "frame", split_axis=2, concat_axis=1, tiled=True)
    frames_all = moved_rows.shape[1]
    sub_places = moved_rows.shape[2]
    flat_rows = moved_rows.reshape(-1, width)
    projected_qkv = (
        jnp.dot(
            flat_rows,
            lax.all_gather(qkv_weight, "frame", axis=1, tiled=True),
            preferred_element_type=jnp.float32,
        )
        .astype(jnp.bfloat16)
        .reshape(2, frames_all, sub_places, 3, width)
    )
    moved = jnp.transpose(projected_qkv, (0, 3, 1, 2, 4))
    frames_all = moved.shape[2]
    sub_places = moved.shape[3]
    arranged = jnp.transpose(moved, (0, 1, 3, 2, 4)).reshape(
        2, 3, sub_places, frames_all, width // HEAD_DIM, HEAD_DIM
    )
    attended = attend(arranged, width // HEAD_DIM)
    attended = jnp.transpose(attended, (0, 2, 1, 3))
    temporal = lax.all_to_all(attended, "frame", split_axis=1, concat_axis=2, tiled=True)
    residual = jnp.stack([hidden, hidden_dot])
    return (residual, temporal)


def lane_window(head):
    low = head * HEAD_DIM // LANES * LANES
    high = -(-(head * HEAD_DIM + HEAD_DIM) // LANES) * LANES
    return low, high


def head_mask(head, low, high):
    lane = lax.broadcasted_iota(jnp.int32, (1, high - low), 1) + low
    return (lane >= head * HEAD_DIM) & (lane < (head + 1) * HEAD_DIM)


def across(left, right):
    return lax.dot_general(left, right, (((1,), (1,)), ((), ())), preferred_element_type=jnp.float32)


def attend_head(mask, query, keys, values, query_dot, keys_dot, values_dot, allowed=None):
    scale = 1.0 / math.sqrt(HEAD_DIM)
    keep = mask.astype(jnp.float32).astype(jnp.bfloat16)
    rows = query.shape[0]
    query = query * keep
    query_dot = query_dot * keep
    both = across(jnp.concatenate([query, query_dot], axis=0), keys)
    scores = both[:rows] * scale
    scores_dot = (both[rows:] + across(query, keys_dot)) * scale
    if allowed is not None:
        scores = jnp.where(allowed, scores, -jnp.inf)
    expo = jnp.exp(scores - jnp.max(scores, axis=-1, keepdims=True))
    probs = expo * (1.0 / jnp.sum(expo, axis=-1, keepdims=True))
    weighted = probs * (scores_dot - jnp.sum(probs * scores_dot, axis=-1, keepdims=True))
    probs_low = probs.astype(jnp.bfloat16)
    stacked = jnp.concatenate([probs_low, weighted.astype(jnp.bfloat16)], axis=0)
    both = jnp.dot(stacked, values, preferred_element_type=jnp.float32)
    output_dot = both[rows:] + jnp.dot(probs_low, values_dot, preferred_element_type=jnp.float32)
    return both[:rows], output_dot


class LaneTiles:
    def __init__(self, heads):
        self.held = {}
        self.last = {}
        for head in range(heads):
            low, high = lane_window(head)
            for tile in range(low // LANES, high // LANES):
                self.last[tile] = head

    def add(self, head, mask, output, output_dot):
        low, high = lane_window(head)
        done = []
        for tile in range(low // LANES, high // LANES):
            part = slice(tile * LANES - low, (tile + 1) * LANES - low)
            here = mask[:, part]
            pair = (output[:, part], output_dot[:, part])
            if tile in self.held:
                pair = tuple(jnp.where(here, a, b) for a, b in zip(pair, self.held[tile]))
            self.held[tile] = pair
            if self.last[tile] == head:
                done.append((tile, self.held.pop(tile)))
        return done


def fused_kernel(
    n, spatial, stream, out_own, qkv_own, mod, residual, returned,
    peer_kv, out_all, qkv_all, attended, rows_send, rows_recv, qkv, back_send,
    kv_sem, own_sem, up_send, down_send, row_send, grid_recv, core_send, core_recv, x_send, x_recv,
    xcore_send, xcore_recv, row_send_sem, row_recv_sem, back_send_sem, back_recv_sem,
):
    clip, core, me = lax.axis_index("clips"), lax.axis_index("pix"), lax.axis_index("frame")
    side = lax.rem(clip, 2)
    x_peer = clip + 1 - 2 * side
    places, width = stream.shape[2], stream.shape[3]
    part = places // n
    heads = width // HEAD_DIM
    half = n // 2

    depth, row = lax.div(me, 2), lax.rem(me, 2)
    depths = n // 2
    to_peer = {"pix": 1 - core}
    to_x = {"clips": x_peer}
    to_row = {"frame": 2 * depth + 1 - row}

    barrier = pltpu.get_barrier_semaphore()
    for target in [to_peer, to_x] + [{"frame": lax.rem(me + k, n)} for k in range(1, n)]:
        pl.semaphore_signal(barrier, inc=1, device_id=target, device_id_type=pl.DeviceIdType.MESH)
    pl.semaphore_wait(barrier, n + 1)

    def remote(source, target, send, recv, device):
        return pltpu.make_async_remote_copy(
            src_ref=source, dst_ref=target, send_sem=send, recv_sem=recv,
            device_id=device, device_id_type=pl.DeviceIdType.MESH,
        )

    kv_copy = remote(spatial.at[:, 1:3, 0], peer_kv, kv_sem.at[0], kv_sem.at[1], to_peer)
    kv_copy.start()

    gathered = (out_all, qkv_all)
    owned = (out_own, qkv_own)
    sizes = tuple(ref.shape[0] for ref in owned)
    my_third = core + (1 - core) * 2 * side
    peer_third = (1 - core) + core * 2 * side
    x_third = 2 * (1 - side)

    def piece(which, frame, third):
        size = sizes[which] // 3
        return gathered[which].at[pl.ds(pl.multiple_of(frame * sizes[which] + third * size, 16), size)]

    def arrives(block, recv):
        return remote(block, block, kv_sem.at[0], recv, to_peer)

    def moves(which, frame, third, send, recv, device):
        block = piece(which, frame, third)
        return remote(block, block, send.at[which, frame], recv.at[which, frame], device)

    def own_move(which, send, device):
        size = sizes[which] // 3
        source = owned[which].at[pl.ds(pl.multiple_of(my_third * size, 16), size)]
        return remote(
            source, piece(which, me, my_third), send.at[which, me], grid_recv.at[which, me], device
        )

    line_copy = lambda which, frame, sign: moves(
        which, frame, my_third, up_send if sign > 0 else down_send, grid_recv, {"frame": me + 2 * sign}
    )
    row_copy = lambda which, frame: moves(which, frame, my_third, row_send, grid_recv, to_row)
    core_copy = lambda which, frame: moves(which, frame, my_third, core_send, core_recv, to_peer)
    x_copy = lambda which, frame: moves(which, frame, my_third, x_send, x_recv, to_x)
    xcore_copy = lambda which, frame: moves(which, frame, x_third, xcore_send, xcore_recv, to_peer)

    def inside(offset):
        return (depth + offset >= 0) & (depth + offset < depths)

    def when_core(which_core, act):
        pl.when(core == which_core)(act)

    def line_step(which, distance):
        for sign in (1, -1):
            @pl.when(inside(-sign * distance))
            def _():
                frame = me - 2 * sign * distance
                arrives(piece(which, frame, my_third), grid_recv.at[which, frame]).wait_recv()

                @pl.when(inside(sign))
                def _():
                    line_copy(which, frame, sign).start()

                row_copy(which, frame).start()
                when_core(0, lambda: x_copy(which, frame).start())
                core_copy(which, frame).start()

    def offsets(distance):
        return (1, -1) if distance else (1,)

    def row_step(which, distance):
        for sign in offsets(distance):
            @pl.when(inside(sign * distance))
            def _():
                frame = 2 * (depth + sign * distance) + 1 - row
                arrives(piece(which, frame, my_third), grid_recv.at[which, frame]).wait_recv()
                when_core(0, lambda: x_copy(which, frame).start())
                core_copy(which, frame).start()

    def x_step(which, distance, turn):
        for sign in offsets(distance):
            @pl.when(inside(sign * distance) & (core == 0))
            def _():
                frame = 2 * (depth + sign * distance) + (1 - turn) * row + turn * (1 - row)
                arrives(piece(which, frame, x_third), x_recv.at[which, frame]).wait_recv()
                xcore_copy(which, frame).start()

    def all_here(which):
        for k in range(1, n):
            frame = lax.rem(me + k, n)
            arrives(piece(which, frame, peer_third), core_recv.at[which, frame]).wait_recv()
            when_core(
                1, lambda: arrives(piece(which, frame, x_third), xcore_recv.at[which, frame]).wait_recv()
            )

    def all_sent(which):
        own_move(which, row_send, to_row).wait_send()
        for sign in (1, -1):
            @pl.when(inside(sign))
            def _():
                own_move(which, up_send if sign > 0 else down_send, {"frame": me + 2 * sign}).wait_send()

            for distance in range(1, depths):
                @pl.when(inside(-sign * distance))
                def _():
                    frame = me - 2 * sign * distance
                    row_copy(which, frame).wait_send()

                    @pl.when(inside(sign))
                    def _():
                        line_copy(which, frame, sign).wait_send()

        for k in range(1, n):
            frame = lax.rem(me + k, n)
            core_copy(which, frame).wait_send()

            @pl.when(core == 0)
            def _():
                x_copy(which, frame).wait_send()
                xcore_copy(which, frame).wait_send()

    own_copies = []
    for which in (0, 1):
        for sign in (1, -1):
            @pl.when(inside(sign))
            def _():
                own_move(which, up_send if sign > 0 else down_send, {"frame": me + 2 * sign}).start()

        own_move(which, row_send, to_row).start()
        whole = gathered[which].at[pl.ds(pl.multiple_of(me * sizes[which], 16), sizes[which])]
        own_copies.append(pltpu.make_async_copy(owned[which], whole, own_sem.at[which]))
        own_copies[-1].start()

    events = []
    for distance in range(depths):
        if distance:
            events.append((2 * distance, line_step, (0, distance)))
            events.append((14 + 4 * (distance - 1), line_step, (1, distance)))
            events.append((2 * distance + 3, x_step, (0, distance, 0)))
            events.append((16 + 5 * (distance - 1), x_step, (1, distance, 0)))
        events.append((2 * distance + 2.5, row_step, (0, distance)))
        events.append((14.5 + 4.5 * distance, row_step, (1, distance)))
        events.append((2 * distance + 5, x_step, (0, distance, 1)))
        events.append((16.5 + 5 * distance, x_step, (1, distance, 1)))
    events.sort(key=lambda event: event[0])

    def serve(until):
        while events and events[0][0] <= until:
            _, act, args = events.pop(0)
            act(*args)

    def serve_all(which):
        for event in [event for event in events if event[2][0] == which]:
            events.remove(event)
            event[1](*event[2])

    kv_copy.wait_recv()
    tiles = LaneTiles(heads)
    for head in range(heads):
        low, high = lane_window(head)
        mask = head_mask(head, low, high)
        both = lambda t, j: jnp.concatenate([spatial[t, 1 + j, 0, :, low:high], peer_kv[t, j, :, low:high]], axis=0)
        output, output_dot = attend_head(
            mask, spatial[0, 0, 0, :, low:high], both(0, 0), both(0, 1),
            spatial[1, 0, 0, :, low:high], both(1, 0), both(1, 1),
        )
        for tile, pair in tiles.add(head, mask, output, output_dot):
            for t in (0, 1):
                attended[t * places:(t + 1) * places, tile * LANES:(tile + 1) * LANES] = pair[t].astype(jnp.bfloat16)
        serve(head + 1)

    serve_all(0)
    all_here(0)
    own_copies[0].wait()

    @pl.loop(0, width // TILE)
    def _(index):
        columns = pl.ds(pl.multiple_of(index * TILE, TILE), TILE)
        projected = across(attended[...], out_all[columns, :])
        gate, gate_slope = mod[0:1, columns], mod[3:4, columns]
        residual[0, 0, :, columns] = stream[0, 0, :, columns].astype(jnp.float32) + gate * projected[:places]
        residual[1, 0, :, columns] = (
            stream[1, 0, :, columns].astype(jnp.float32)
            + gate_slope * projected[:places]
            + gate * projected[places:]
        )

    serve(17)
    row_copies = []
    for k in list(range(1, n)) + [0]:
        frame = lax.rem(me + k, n)
        rows = pl.ds(pl.multiple_of(frame * part, 8), part)
        hidden, hidden_dot = residual[0, 0, rows, :], residual[1, 0, rows, :]
        centered = hidden - jnp.mean(hidden, axis=-1, keepdims=True)
        inv_scale = lax.rsqrt(jnp.mean(centered * centered, axis=-1, keepdims=True) + 1e-06)
        normed = centered * inv_scale
        normed_dot = (
            hidden_dot
            - jnp.mean(hidden_dot, axis=-1, keepdims=True)
            - normed * jnp.mean(normed * hidden_dot, axis=-1, keepdims=True)
        ) * inv_scale
        modulated = normed * (1.0 + mod[2:3, :]) + mod[1:2, :]
        modulated_dot = normed_dot * (1.0 + mod[2:3, :]) + normed * mod[5:6, :] + mod[4:5, :]
        block = jnp.concatenate([modulated, modulated_dot], axis=0).astype(jnp.bfloat16)
        mine = pl.ds(pl.multiple_of(me * 2 * part, 16), 2 * part)
        if k == 0:
            rows_recv[mine, :] = block
        else:
            theirs = pl.ds(pl.multiple_of(frame * 2 * part, 16), 2 * part)
            rows_send[theirs, :] = block
            row_copies.append(remote(
                rows_send.at[theirs], rows_recv.at[mine], row_send_sem.at[k], row_recv_sem.at[k], {"frame": frame}
            ))
            row_copies[-1].start()

    serve_all(1)
    all_here(1)
    own_copies[1].wait()
    for k in range(1, n):
        source = lax.rem(me - k + n, n)
        arrives(rows_recv.at[pl.ds(pl.multiple_of(source * 2 * part, 16), 2 * part)], row_recv_sem.at[k]).wait_recv()

    def project_chunk(chunk):
        @pl.loop(0, 3)
        def _(index):
            columns = pl.ds(pl.multiple_of(index * width + chunk * TILE, LANES), TILE)
            product = across(rows_recv[...], qkv_all[columns, :])
            for t in (0, 1):
                kept = [product[(2 * f + t) * part:(2 * f + t + 1) * part] for f in range(n)]
                qkv[t, :, columns] = jnp.concatenate(kept, axis=0).astype(jnp.bfloat16)

    rows = n * part
    one = lax.rem(lax.broadcasted_iota(jnp.int32, (rows, rows), 0), part)
    two = lax.rem(lax.broadcasted_iota(jnp.int32, (rows, rows), 1), part)
    allowed = one == two
    tiles = LaneTiles(heads)
    chunks = back_send.shape[0]
    chunk_tiles = width // LANES // chunks
    back_copies = []
    pieces = {}
    ready = 0
    for head in range(heads):
        low, high = lane_window(head)
        while ready * TILE < high:
            project_chunk(ready)
            ready += 1
        mask = head_mask(head, low, high)
        take = lambda t, j: qkv[t, :, j * width + low:j * width + high]
        output, output_dot = attend_head(
            mask, take(0, 0), take(0, 1), take(0, 2), take(1, 0), take(1, 1), take(1, 2), allowed
        )
        for tile, pair in tiles.add(head, mask, output, output_dot):
            chunk, inner = tile // chunk_tiles, tile % chunk_tiles
            for f in range(n):
                block = jnp.concatenate([value[f * part:(f + 1) * part] for value in pair], axis=0)
                back_send[chunk, f, :, inner * LANES:(inner + 1) * LANES] = block.astype(jnp.bfloat16)
            if inner == chunk_tiles - 1:
                own = pltpu.make_async_copy(
                    back_send.at[chunk, me], returned.at[chunk, me], back_send_sem.at[chunk, 0]
                )
                own.start()
                back_copies.append(own)
                for k in range(1, n):
                    frame = lax.rem(me + k, n)
                    copy = remote(
                        back_send.at[chunk, frame], returned.at[chunk, me],
                        back_send_sem.at[chunk, k], back_recv_sem.at[chunk, k], {"frame": frame},
                    )
                    copy.start()
                    pieces[chunk, k] = copy

    kv_copy.wait_send()
    for which in (0, 1):
        all_sent(which)
    for copy in row_copies:
        copy.wait_send()
    for copy in back_copies:
        copy.wait()
    for (chunk, k), copy in pieces.items():
        copy.wait_send()
        source = lax.rem(me - k + n, n)
        arrives(returned.at[chunk, source], back_recv_sem.at[chunk, k]).wait_recv()


def finish_kernel(residual, returned, residual_out, temporal_out, blocks, temporal, sem):
    chunks, n, rows, tile = returned.shape
    part = rows // 2
    arrivals = [pltpu.make_async_copy(returned.at[c], blocks.at[c], sem.at[c]) for c in range(chunks)]
    leaving = [pltpu.make_async_copy(residual.at[t], residual_out.at[t], sem.at[2 * chunks + t]) for t in (0, 1)]
    for copy in arrivals + leaving:
        copy.start()
    for chunk in range(chunks):
        arrivals[chunk].wait()
        for f in range(n):
            block = blocks[chunk, f].astype(jnp.float32)
            for t in (0, 1):
                temporal[t, 0, f * part:(f + 1) * part, chunk * tile:(chunk + 1) * tile] = (
                    block[t * part:(t + 1) * part]
                )
        columns = pl.ds(chunk * tile, tile)
        leaving.append(pltpu.make_async_copy(
            temporal.at[:, :, :, columns], temporal_out.at[:, :, :, columns], sem.at[chunks + chunk]
        ))
        leaving[-1].start()
    for copy in leaving:
        copy.wait()


def per_device_fused(n, stream, spatial_qkv, out_weight, qkv_weight, mod_table, timestep):
    places, width = stream.shape[2], stream.shape[3]
    part = places // n
    chunks = width // TILE
    mod = jnp.concatenate(modulation(mod_table, timestep), axis=0)
    bf16, f32 = jnp.bfloat16, jnp.float32
    dma = pltpu.SemaphoreType.DMA
    vmem = pl.BlockSpec(memory_space=pltpu.VMEM)
    residual, returned = pl.pallas_call(
        functools.partial(fused_kernel, n),
        out_shape=(
            jax.ShapeDtypeStruct(stream.shape, f32),
            jax.ShapeDtypeStruct((chunks, n, 2 * part, TILE), bf16),
        ),
        in_specs=[vmem] * 5,
        out_specs=(vmem, vmem),
        scratch_shapes=[
            pltpu.VMEM((2, 2, places, width), bf16),
            pltpu.VMEM((width, width), bf16),
            pltpu.VMEM((3 * width, width), bf16),
            pltpu.VMEM((2 * places, width), bf16),
            pltpu.VMEM((2 * places, width), bf16),
            pltpu.VMEM((2 * places, width), bf16),
            pltpu.VMEM((2, places, 3 * width), bf16),
            pltpu.VMEM((chunks, n, 2 * part, TILE), bf16),
            dma((2,)), dma((2,)),
        ] + [dma((2, n))] * 10 + [dma((n,))] * 2 + [dma((chunks, n))] * 2,
        compiler_params=pltpu.CompilerParams(
            collective_id=0, has_side_effects=True, vmem_limit_bytes=56 * 1024 * 1024
        ),
    )(spatial_qkv, stream, out_weight.T, qkv_weight.T, mod)
    return tuple(pl.pallas_call(
        finish_kernel,
        out_shape=(jax.ShapeDtypeStruct(stream.shape, f32),) * 2,
        in_specs=[pl.BlockSpec(memory_space=pl.ANY)] * 2,
        out_specs=(pl.BlockSpec(memory_space=pl.ANY),) * 2,
        scratch_shapes=[
            pltpu.VMEM((chunks, n, 2 * part, TILE), bf16), pltpu.VMEM(stream.shape, f32), dma((2 * chunks + 2,))
        ],
        compiler_params=pltpu.CompilerParams(vmem_limit_bytes=56 * 1024 * 1024),
    )(residual, returned))


def fits_fused(mesh, places, width, out_columns, qkv_columns, frames_local):
    n = mesh.shape["frame"]
    return (
        mesh.shape["pix"] == 2
        and mesh.shape["clips"] % 2 == 0
        and n % 2 == 0
        and frames_local == 1
        and places % n == 0
        and (places // n) % 8 == 0
        and places % 16 == 0
        and width % TILE == 0
        and width % HEAD_DIM == 0
        and out_columns % 48 == 0
        and qkv_columns % 48 == 0
    )


def solution(mesh):
    in_specs = (
        P(None, ("clips", "frame"), "pix", None),
        P(None, None, ("clips", "frame"), "pix", None),
        P(None, "frame"),
        P(None, "frame"),
        P(),
        P("clips"),
    )
    out_specs = (P(None, ("clips", "frame"), "pix", None), P(None, ("clips", "frame"), "pix", None))

    def local(stream, spatial_qkv, out_weight, qkv_weight, mod_table, timestep):
        args = (stream, spatial_qkv, out_weight, qkv_weight, mod_table, timestep)
        if fits_fused(
            mesh, stream.shape[2], stream.shape[3], out_weight.shape[1], qkv_weight.shape[1], stream.shape[1]
        ):
            return per_device_fused(mesh.shape["frame"], *args)
        return per_device(*args)

    return jax.shard_map(local, mesh=mesh, in_specs=in_specs, out_specs=out_specs, check_vma=False)
```

```python
import functools
import math

import jax
import jax.numpy as jnp
from jax import lax
from jax.experimental import pallas as pl
from jax.experimental.pallas import tpu as pltpu
from jax.sharding import PartitionSpec as P

HEAD_DIM = 72
LANES = 128
TILE = 384


def modulation(mod_table, timestep):
    width = mod_table.shape[-1]
    frequency = jnp.exp(-math.log(10.0) * jnp.arange(width).astype(jnp.float32) / width)
    time_value = timestep[0].astype(jnp.float32) * (math.pi / 1000.0)
    mod_value = mod_table[:, 0] + mod_table[:, 1] * jnp.cos(frequency * time_value)
    mod_slope = -mod_table[:, 1] * frequency * jnp.sin(frequency * time_value)
    return (mod_value, mod_slope)


def attend_group(inputs):
    query, keys, values, query_dot, keys_dot, values_dot = inputs
    scale = 1.0 / math.sqrt(query.shape[-1])
    scores = jnp.einsum("blhe,bmhe->bhlm", query, keys, preferred_element_type=jnp.float32) * scale
    scores_dot = (
        jnp.einsum("blhe,bmhe->bhlm", query_dot, keys, preferred_element_type=jnp.float32)
        + jnp.einsum("blhe,bmhe->bhlm", query, keys_dot, preferred_element_type=jnp.float32)
    ) * scale
    top_score = jnp.max(scores, axis=-1, keepdims=True)
    expo = jnp.exp(scores - top_score)
    probs = expo / jnp.sum(expo, axis=-1, keepdims=True)
    probs_low = probs.astype(jnp.bfloat16)
    output = jnp.einsum("bhlm,bmhe->blhe", probs_low, values, preferred_element_type=jnp.float32)
    row_total = jnp.sum(probs * scores_dot, axis=-1, keepdims=True)
    weighted = probs * (scores_dot - row_total)
    weighted_low = weighted.astype(jnp.bfloat16)
    output_dot = jnp.einsum(
        "bhlm,bmhe->blhe", weighted_low, values, preferred_element_type=jnp.float32
    ) + jnp.einsum("bhlm,bmhe->blhe", probs_low, values_dot, preferred_element_type=jnp.float32)
    return (output, output_dot)


def attend(stacked, group_size):
    batch, length, heads_all, head_size = stacked.shape[2:]
    groups = heads_all // group_size
    shaped = stacked.reshape(2, 3, batch, length, groups, group_size, head_size)
    shaped = jnp.transpose(shaped, (4, 0, 1, 2, 3, 5, 6))
    inputs = (
        shaped[:, 0, 0],
        shaped[:, 0, 1],
        shaped[:, 0, 2],
        shaped[:, 1, 0],
        shaped[:, 1, 1],
        shaped[:, 1, 2],
    )
    output, output_dot = lax.map(attend_group, inputs)
    joined = jnp.stack([output, output_dot], axis=1)
    joined = jnp.transpose(joined, (1, 2, 3, 0, 4, 5))
    return joined.reshape(2, batch, length, heads_all * head_size)


def per_device(stream, spatial_qkv, out_weight, qkv_weight, mod_table, timestep):
    frames_local = stream.shape[1]
    places = stream.shape[2]
    width = stream.shape[3]
    block = lax.all_to_all(spatial_qkv, "pix", split_axis=4, concat_axis=3, tiled=True)
    frames_here = block.shape[2]
    length = block.shape[3]
    channels = block.shape[4]
    shaped = block.reshape(2, 3, frames_here, length, channels // HEAD_DIM, HEAD_DIM)
    attended = attend(shaped, 1).astype(jnp.bfloat16)
    spatial = lax.all_to_all(attended, "pix", split_axis=2, concat_axis=3, tiled=True)
    flat_spatial = spatial.reshape(-1, width)
    projected = jnp.dot(
        flat_spatial,
        lax.all_gather(out_weight, "frame", axis=1, tiled=True),
        preferred_element_type=jnp.float32,
    )
    projected = projected.reshape(2, frames_local, places, width)
    mod_value, mod_slope = modulation(mod_table, timestep)
    primal_in = stream[0].astype(jnp.float32)
    tangent_in = stream[1].astype(jnp.float32)
    hidden = primal_in + mod_value[0] * projected[0]
    hidden_dot = tangent_in + mod_slope[0] * projected[0] + mod_value[0] * projected[1]
    centered = hidden - jnp.mean(hidden, axis=-1, keepdims=True)
    inv_scale = lax.rsqrt(jnp.mean(centered * centered, axis=-1, keepdims=True) + 1e-06)
    normed = centered * inv_scale
    normed_dot = (
        hidden_dot
        - jnp.mean(hidden_dot, axis=-1, keepdims=True)
        - normed * jnp.mean(normed * hidden_dot, axis=-1, keepdims=True)
    ) * inv_scale
    modulated = normed * (1.0 + mod_value[2]) + mod_value[1]
    modulated_dot = normed_dot * (1.0 + mod_value[2]) + normed * mod_slope[2] + mod_slope[1]
    modulated_low = jnp.stack([modulated, modulated_dot]).astype(jnp.bfloat16)
    moved_rows = lax.all_to_all(modulated_low, "frame", split_axis=2, concat_axis=1, tiled=True)
    frames_all = moved_rows.shape[1]
    sub_places = moved_rows.shape[2]
    flat_rows = moved_rows.reshape(-1, width)
    projected_qkv = (
        jnp.dot(
            flat_rows,
            lax.all_gather(qkv_weight, "frame", axis=1, tiled=True),
            preferred_element_type=jnp.float32,
        )
        .astype(jnp.bfloat16)
        .reshape(2, frames_all, sub_places, 3, width)
    )
    moved = jnp.transpose(projected_qkv, (0, 3, 1, 2, 4))
    frames_all = moved.shape[2]
    sub_places = moved.shape[3]
    arranged = jnp.transpose(moved, (0, 1, 3, 2, 4)).reshape(
        2, 3, sub_places, frames_all, width // HEAD_DIM, HEAD_DIM
    )
    attended = attend(arranged, width // HEAD_DIM)
    attended = jnp.transpose(attended, (0, 2, 1, 3))
    temporal = lax.all_to_all(attended, "frame", split_axis=1, concat_axis=2, tiled=True)
    residual = jnp.stack([hidden, hidden_dot])
    return (residual, temporal)


def lane_window(head):
    low = head * HEAD_DIM // LANES * LANES
    high = -(-(head * HEAD_DIM + HEAD_DIM) // LANES) * LANES
    return low, high


def head_mask(head, low, high):
    lane = lax.broadcasted_iota(jnp.int32, (1, high - low), 1) + low
    return (lane >= head * HEAD_DIM) & (lane < (head + 1) * HEAD_DIM)


def across(left, right):
    return lax.dot_general(left, right, (((1,), (1,)), ((), ())), preferred_element_type=jnp.float32)


def attend_head(mask, query, keys, values, query_dot, keys_dot, values_dot, allowed=None):
    scale = 1.0 / math.sqrt(HEAD_DIM)
    keep = mask.astype(jnp.float32).astype(jnp.bfloat16)
    rows = query.shape[0]
    query = query * keep
    query_dot = query_dot * keep
    both = across(jnp.concatenate([query, query_dot], axis=0), keys)
    scores = both[:rows]
    scores_dot = both[rows:] + across(query, keys_dot)
    if allowed is not None:
        scores = jnp.where(allowed, scores, -jnp.inf)
    expo = jnp.exp((scores - jnp.max(scores, axis=-1, keepdims=True)) * scale)
    inverse = 1.0 / jnp.sum(expo, axis=-1, keepdims=True)
    weighted = expo * (scores_dot - inverse * jnp.sum(expo * scores_dot, axis=-1, keepdims=True))
    expo_low = expo.astype(jnp.bfloat16)
    stacked = jnp.concatenate([expo_low, weighted.astype(jnp.bfloat16)], axis=0)
    both = jnp.dot(stacked, values, preferred_element_type=jnp.float32)
    output_dot = both[rows:] * scale + jnp.dot(expo_low, values_dot, preferred_element_type=jnp.float32)
    return both[:rows] * inverse, output_dot * inverse


class LaneTiles:
    def __init__(self, heads):
        self.held = {}
        self.last = {}
        for head in range(heads):
            low, high = lane_window(head)
            for tile in range(low // LANES, high // LANES):
                self.last[tile] = head

    def add(self, head, mask, output, output_dot):
        low, high = lane_window(head)
        done = []
        for tile in range(low // LANES, high // LANES):
            part = slice(tile * LANES - low, (tile + 1) * LANES - low)
            here = mask[:, part]
            pair = (output[:, part], output_dot[:, part])
            if tile in self.held:
                pair = tuple(jnp.where(here, a, b) for a, b in zip(pair, self.held[tile]))
            self.held[tile] = pair
            if self.last[tile] == head:
                done.append((tile, self.held.pop(tile)))
        return done


def fused_kernel(
    n, spatial_in, stream_in, out_own, qkv_own, mod, residual_out, returned,
    spatial, stream, residual, in_sem, peer_kv, out_all, qkv_all, attended, rows_send, rows_recv, qkv, back_send,
    kv_sem, own_sem, up_send, down_send, row_send, grid_recv, core_send, core_recv, x_send, x_recv,
    xcore_send, xcore_recv, row_send_sem, row_recv_sem, back_send_sem, back_recv_sem,
):
    clip, core, me = lax.axis_index("clips"), lax.axis_index("pix"), lax.axis_index("frame")
    side = lax.rem(clip, 2)
    x_peer = clip + 1 - 2 * side
    places, width = stream.shape[2], stream.shape[3]
    part = places // n
    heads = width // HEAD_DIM
    half = n // 2

    depth, row = lax.div(me, 2), lax.rem(me, 2)
    depths = n // 2
    to_peer = {"pix": 1 - core}
    to_x = {"clips": x_peer}
    to_row = {"frame": 2 * depth + 1 - row}

    spatial_copy = pltpu.make_async_copy(spatial_in, spatial, in_sem.at[0])
    stream_copy = pltpu.make_async_copy(stream_in, stream, in_sem.at[1])
    spatial_copy.start()

    barrier = pltpu.get_barrier_semaphore()
    for target in [to_peer, to_x] + [{"frame": lax.rem(me + k, n)} for k in range(1, n)]:
        pl.semaphore_signal(barrier, inc=1, device_id=target, device_id_type=pl.DeviceIdType.MESH)
    pl.semaphore_wait(barrier, n + 1)

    def remote(source, target, send, recv, device):
        return pltpu.make_async_remote_copy(
            src_ref=source, dst_ref=target, send_sem=send, recv_sem=recv,
            device_id=device, device_id_type=pl.DeviceIdType.MESH,
        )

    kv_copy = remote(spatial_in.at[:, 1:3, 0], peer_kv, kv_sem.at[0], kv_sem.at[1], to_peer)
    kv_copy.start()

    gathered = (out_all, qkv_all)
    owned = (out_own, qkv_own)
    sizes = tuple(ref.shape[0] for ref in owned)
    my_third = core + (1 - core) * 2 * side
    peer_third = (1 - core) + core * 2 * side
    x_third = 2 * (1 - side)

    def piece(which, frame, third):
        size = sizes[which] // 3
        return gathered[which].at[pl.ds(pl.multiple_of(frame * sizes[which] + third * size, 16), size)]

    def arrives(block, recv):
        return remote(block, block, kv_sem.at[0], recv, to_peer)

    def moves(which, frame, third, send, recv, device):
        block = piece(which, frame, third)
        return remote(block, block, send.at[which, frame], recv.at[which, frame], device)

    def own_move(which, send, device):
        size = sizes[which] // 3
        source = owned[which].at[pl.ds(pl.multiple_of(my_third * size, 16), size)]
        return remote(
            source, piece(which, me, my_third), send.at[which, me], grid_recv.at[which, me], device
        )

    line_copy = lambda which, frame, sign: moves(
        which, frame, my_third, up_send if sign > 0 else down_send, grid_recv, {"frame": me + 2 * sign}
    )
    row_copy = lambda which, frame: moves(which, frame, my_third, row_send, grid_recv, to_row)
    core_copy = lambda which, frame: moves(which, frame, my_third, core_send, core_recv, to_peer)
    x_copy = lambda which, frame: moves(which, frame, my_third, x_send, x_recv, to_x)
    xcore_copy = lambda which, frame: moves(which, frame, x_third, xcore_send, xcore_recv, to_peer)

    def inside(offset):
        return (depth + offset >= 0) & (depth + offset < depths)

    def when_core(which_core, act):
        pl.when(core == which_core)(act)

    def line_step(which, distance):
        for sign in (1, -1):
            @pl.when(inside(-sign * distance))
            def _():
                frame = me - 2 * sign * distance
                arrives(piece(which, frame, my_third), grid_recv.at[which, frame]).wait_recv()

                @pl.when(inside(sign))
                def _():
                    line_copy(which, frame, sign).start()

                row_copy(which, frame).start()
                when_core(0, lambda: x_copy(which, frame).start())
                core_copy(which, frame).start()

    def offsets(distance):
        return (1, -1) if distance else (1,)

    def row_step(which, distance):
        for sign in offsets(distance):
            @pl.when(inside(sign * distance))
            def _():
                frame = 2 * (depth + sign * distance) + 1 - row
                arrives(piece(which, frame, my_third), grid_recv.at[which, frame]).wait_recv()
                when_core(0, lambda: x_copy(which, frame).start())
                core_copy(which, frame).start()

    def x_step(which, distance, turn):
        for sign in offsets(distance):
            @pl.when(inside(sign * distance) & (core == 0))
            def _():
                frame = 2 * (depth + sign * distance) + (1 - turn) * row + turn * (1 - row)
                arrives(piece(which, frame, x_third), x_recv.at[which, frame]).wait_recv()
                xcore_copy(which, frame).start()

    def all_here(which):
        for k in range(1, n):
            frame = lax.rem(me + k, n)
            arrives(piece(which, frame, peer_third), core_recv.at[which, frame]).wait_recv()
            when_core(
                1, lambda: arrives(piece(which, frame, x_third), xcore_recv.at[which, frame]).wait_recv()
            )

    def all_sent(which):
        own_move(which, row_send, to_row).wait_send()
        for sign in (1, -1):
            @pl.when(inside(sign))
            def _():
                own_move(which, up_send if sign > 0 else down_send, {"frame": me + 2 * sign}).wait_send()

            for distance in range(1, depths):
                @pl.when(inside(-sign * distance))
                def _():
                    frame = me - 2 * sign * distance
                    row_copy(which, frame).wait_send()

                    @pl.when(inside(sign))
                    def _():
                        line_copy(which, frame, sign).wait_send()

        for k in range(1, n):
            frame = lax.rem(me + k, n)
            core_copy(which, frame).wait_send()

            @pl.when(core == 0)
            def _():
                x_copy(which, frame).wait_send()
                xcore_copy(which, frame).wait_send()

    own_copies = []
    for which in (0, 1):
        for sign in (1, -1):
            @pl.when(inside(sign))
            def _():
                own_move(which, up_send if sign > 0 else down_send, {"frame": me + 2 * sign}).start()

        own_move(which, row_send, to_row).start()
        whole = gathered[which].at[pl.ds(pl.multiple_of(me * sizes[which], 16), sizes[which])]
        own_copies.append(pltpu.make_async_copy(owned[which], whole, own_sem.at[which]))
        own_copies[-1].start()
    stream_copy.start()

    events = []
    for distance in range(depths):
        if distance:
            events.append((2 * distance, line_step, (0, distance)))
            events.append((4 * distance + 1, line_step, (1, distance)))
            events.append((2 * distance + 3, x_step, (0, distance, 0)))
            events.append((4 * distance + 6, x_step, (1, distance, 0)))
        events.append((2 * distance + 2.5, row_step, (0, distance)))
        events.append((4 * distance + 5, row_step, (1, distance)))
        events.append((2 * distance + 5, x_step, (0, distance, 1)))
        events.append((4 * distance + 8, x_step, (1, distance, 1)))
    events.sort(key=lambda event: event[0])

    def serve(until):
        while events and events[0][0] <= until:
            _, act, args = events.pop(0)
            act(*args)

    def serve_all(which):
        for event in [event for event in events if event[2][0] == which]:
            events.remove(event)
            event[1](*event[2])

    spatial_copy.wait()
    kv_copy.wait_recv()
    tiles = LaneTiles(heads)
    for head in range(heads):
        low, high = lane_window(head)
        mask = head_mask(head, low, high)
        both = lambda t, j: jnp.concatenate([spatial[t, 1 + j, 0, :, low:high], peer_kv[t, j, :, low:high]], axis=0)
        output, output_dot = attend_head(
            mask, spatial[0, 0, 0, :, low:high], both(0, 0), both(0, 1),
            spatial[1, 0, 0, :, low:high], both(1, 0), both(1, 1),
        )
        for tile, pair in tiles.add(head, mask, output, output_dot):
            for t in (0, 1):
                attended[t * places:(t + 1) * places, tile * LANES:(tile + 1) * LANES] = pair[t].astype(jnp.bfloat16)
        serve(head + 1)

    serve_all(0)
    all_here(0)
    own_copies[0].wait()
    stream_copy.wait()

    @pl.loop(0, width // TILE)
    def _(index):
        columns = pl.ds(pl.multiple_of(index * TILE, TILE), TILE)
        projected = across(attended[...], out_all[columns, :])
        gate, gate_slope = mod[0:1, columns], mod[3:4, columns]
        residual[0, 0, :, columns] = stream[0, 0, :, columns].astype(jnp.float32) + gate * projected[:places]
        residual[1, 0, :, columns] = (
            stream[1, 0, :, columns].astype(jnp.float32)
            + gate_slope * projected[:places]
            + gate * projected[places:]
        )

    serve(17)
    row_copies = []
    for k in list(range(1, n)) + [0]:
        frame = lax.rem(me + k, n)
        rows = pl.ds(pl.multiple_of(frame * part, 8), part)
        hidden, hidden_dot = residual[0, 0, rows, :], residual[1, 0, rows, :]
        centered = hidden - jnp.mean(hidden, axis=-1, keepdims=True)
        inv_scale = lax.rsqrt(jnp.mean(centered * centered, axis=-1, keepdims=True) + 1e-06)
        normed = centered * inv_scale
        normed_dot = (
            hidden_dot
            - jnp.mean(hidden_dot, axis=-1, keepdims=True)
            - normed * jnp.mean(normed * hidden_dot, axis=-1, keepdims=True)
        ) * inv_scale
        modulated = normed * (1.0 + mod[2:3, :]) + mod[1:2, :]
        modulated_dot = normed_dot * (1.0 + mod[2:3, :]) + normed * mod[5:6, :] + mod[4:5, :]
        block = jnp.concatenate([modulated, modulated_dot], axis=0).astype(jnp.bfloat16)
        mine = pl.ds(pl.multiple_of(me * 2 * part, 16), 2 * part)
        if k == 0:
            rows_recv[mine, :] = block
        else:
            theirs = pl.ds(pl.multiple_of(frame * 2 * part, 16), 2 * part)
            rows_send[theirs, :] = block
            row_copies.append(remote(
                rows_send.at[theirs], rows_recv.at[mine], row_send_sem.at[k], row_recv_sem.at[k], {"frame": frame}
            ))
            row_copies[-1].start()
        serve(18 + k)

    residual_copy = pltpu.make_async_copy(residual, residual_out, in_sem.at[2])
    residual_copy.start()
    serve_all(1)
    all_here(1)
    own_copies[1].wait()
    for k in range(1, n):
        source = lax.rem(me - k + n, n)
        arrives(rows_recv.at[pl.ds(pl.multiple_of(source * 2 * part, 16), 2 * part)], row_recv_sem.at[k]).wait_recv()

    def project_chunk(chunk):
        @pl.loop(0, 3)
        def _(index):
            columns = pl.ds(pl.multiple_of(index * width + chunk * TILE, LANES), TILE)
            product = across(rows_recv[...], qkv_all[columns, :])
            for t in (0, 1):
                kept = [product[(2 * f + t) * part:(2 * f + t + 1) * part] for f in range(n)]
                qkv[t, :, columns] = jnp.concatenate(kept, axis=0).astype(jnp.bfloat16)

    rows = n * part
    one = lax.rem(lax.broadcasted_iota(jnp.int32, (rows, rows), 0), part)
    two = lax.rem(lax.broadcasted_iota(jnp.int32, (rows, rows), 1), part)
    allowed = one == two
    tiles = LaneTiles(heads)
    chunks = back_send.shape[0]
    chunk_tiles = width // LANES // chunks
    back_copies = []
    pieces = {}
    ready = 0
    for head in range(heads):
        low, high = lane_window(head)
        while ready * TILE < high:
            project_chunk(ready)
            ready += 1
        mask = head_mask(head, low, high)
        take = lambda t, j: qkv[t, :, j * width + low:j * width + high]
        output, output_dot = attend_head(
            mask, take(0, 0), take(0, 1), take(0, 2), take(1, 0), take(1, 1), take(1, 2), allowed
        )
        for tile, pair in tiles.add(head, mask, output, output_dot):
            chunk, inner = tile // chunk_tiles, tile % chunk_tiles
            for f in range(n):
                block = jnp.concatenate([value[f * part:(f + 1) * part] for value in pair], axis=0)
                back_send[chunk, f, :, inner * LANES:(inner + 1) * LANES] = block.astype(jnp.bfloat16)
            if inner == chunk_tiles - 1:
                own = pltpu.make_async_copy(
                    back_send.at[chunk, me], returned.at[chunk, me], back_send_sem.at[chunk, 0]
                )
                own.start()
                back_copies.append(own)
                for k in range(1, n):
                    frame = lax.rem(me + k, n)
                    copy = remote(
                        back_send.at[chunk, frame], returned.at[chunk, me],
                        back_send_sem.at[chunk, k], back_recv_sem.at[chunk, k], {"frame": frame},
                    )
                    copy.start()
                    pieces[chunk, k] = copy

    residual_copy.wait()
    kv_copy.wait_send()
    for which in (0, 1):
        all_sent(which)
    for copy in row_copies:
        copy.wait_send()
    for copy in back_copies:
        copy.wait()
    for (chunk, k), copy in pieces.items():
        copy.wait_send()
        source = lax.rem(me - k + n, n)
        arrives(returned.at[chunk, source], back_recv_sem.at[chunk, k]).wait_recv()


def finish_kernel(residual, returned, residual_out, temporal_out, blocks, held, temporal, sem):
    chunks, n, rows, tile = returned.shape
    part = rows // 2
    arrivals = [pltpu.make_async_copy(returned.at[c], blocks.at[c], sem.at[c]) for c in range(chunks)]
    passing = [pltpu.make_async_copy(residual.at[t], held.at[t], sem.at[2 * chunks + t]) for t in (0, 1)]
    for copy in arrivals + passing:
        copy.start()
    leaving = []
    for chunk in range(chunks):
        arrivals[chunk].wait()
        for f in range(n):
            block = blocks[chunk, f].astype(jnp.float32)
            for t in (0, 1):
                temporal[t, 0, f * part:(f + 1) * part, chunk * tile:(chunk + 1) * tile] = (
                    block[t * part:(t + 1) * part]
                )
        columns = pl.ds(chunk * tile, tile)
        leaving.append(pltpu.make_async_copy(
            temporal.at[:, :, :, columns], temporal_out.at[:, :, :, columns], sem.at[chunks + chunk]
        ))
        leaving[-1].start()
        if chunk < 2:
            passing[chunk].wait()
            leaving.append(pltpu.make_async_copy(
                held.at[chunk], residual_out.at[chunk], sem.at[2 * chunks + 2 + chunk]
            ))
            leaving[-1].start()
    for copy in leaving:
        copy.wait()


def per_device_fused(n, stream, spatial_qkv, out_weight, qkv_weight, mod_table, timestep):
    places, width = stream.shape[2], stream.shape[3]
    part = places // n
    chunks = width // TILE
    mod = jnp.concatenate(modulation(mod_table, timestep), axis=0)
    bf16, f32 = jnp.bfloat16, jnp.float32
    dma = pltpu.SemaphoreType.DMA
    vmem = pl.BlockSpec(memory_space=pltpu.VMEM)
    anywhere = pl.BlockSpec(memory_space=pl.ANY)
    residual, returned = pl.pallas_call(
        functools.partial(fused_kernel, n),
        out_shape=(
            jax.ShapeDtypeStruct(stream.shape, f32),
            jax.ShapeDtypeStruct((chunks, n, 2 * part, TILE), bf16),
        ),
        in_specs=[anywhere] * 4 + [vmem],
        out_specs=(anywhere, vmem),
        scratch_shapes=[
            pltpu.VMEM(spatial_qkv.shape, bf16),
            pltpu.VMEM(stream.shape, bf16),
            pltpu.VMEM(stream.shape, f32),
            dma((3,)),
            pltpu.VMEM((2, 2, places, width), bf16),
            pltpu.VMEM((width, width), bf16),
            pltpu.VMEM((3 * width, width), bf16),
            pltpu.VMEM((2 * places, width), bf16),
            pltpu.VMEM((2 * places, width), bf16),
            pltpu.VMEM((2 * places, width), bf16),
            pltpu.VMEM((2, places, 3 * width), bf16),
            pltpu.VMEM((chunks, n, 2 * part, TILE), bf16),
            dma((2,)), dma((2,)),
        ] + [dma((2, n))] * 10 + [dma((n,))] * 2 + [dma((chunks, n))] * 2,
        compiler_params=pltpu.CompilerParams(
            collective_id=0, has_side_effects=True, vmem_limit_bytes=56 * 1024 * 1024
        ),
    )(spatial_qkv, stream, out_weight.T, qkv_weight.T, mod)
    return tuple(pl.pallas_call(
        finish_kernel,
        out_shape=(jax.ShapeDtypeStruct(stream.shape, f32),) * 2,
        in_specs=[anywhere] * 2,
        out_specs=(anywhere,) * 2,
        scratch_shapes=[
            pltpu.VMEM((chunks, n, 2 * part, TILE), bf16),
            pltpu.VMEM(stream.shape, f32),
            pltpu.VMEM(stream.shape, f32),
            dma((2 * chunks + 4,)),
        ],
        compiler_params=pltpu.CompilerParams(vmem_limit_bytes=56 * 1024 * 1024),
    )(residual, returned))


def fits_fused(mesh, places, width, out_columns, qkv_columns, frames_local):
    n = mesh.shape["frame"]
    return (
        mesh.shape["pix"] == 2
        and mesh.shape["clips"] % 2 == 0
        and n % 2 == 0
        and frames_local == 1
        and places % n == 0
        and (places // n) % 8 == 0
        and places % 16 == 0
        and width % TILE == 0
        and width >= 2 * TILE
        and width % HEAD_DIM == 0
        and out_columns % 48 == 0
        and qkv_columns % 48 == 0
    )


def solution(mesh):
    in_specs = (
        P(None, ("clips", "frame"), "pix", None),
        P(None, None, ("clips", "frame"), "pix", None),
        P(None, "frame"),
        P(None, "frame"),
        P(),
        P("clips"),
    )
    out_specs = (P(None, ("clips", "frame"), "pix", None), P(None, ("clips", "frame"), "pix", None))

    def local(stream, spatial_qkv, out_weight, qkv_weight, mod_table, timestep):
        args = (stream, spatial_qkv, out_weight, qkv_weight, mod_table, timestep)
        if fits_fused(
            mesh, stream.shape[2], stream.shape[3], out_weight.shape[1], qkv_weight.shape[1], stream.shape[1]
        ):
            return per_device_fused(mesh.shape["frame"], *args)
        return per_device(*args)

    return jax.shard_map(local, mesh=mesh, in_specs=in_specs, out_specs=out_specs, check_vma=False)
```

```python
import functools
import math

import jax
import jax.numpy as jnp
from jax import lax
from jax.experimental import pallas as pl
from jax.experimental.pallas import tpu as pltpu
from jax.sharding import PartitionSpec as P

HEAD_DIM = 72
LANES = 128
TILE = 384


def modulation(mod_table, timestep):
    width = mod_table.shape[-1]
    frequency = jnp.exp(-math.log(10.0) * jnp.arange(width).astype(jnp.float32) / width)
    time_value = timestep[0].astype(jnp.float32) * (math.pi / 1000.0)
    mod_value = mod_table[:, 0] + mod_table[:, 1] * jnp.cos(frequency * time_value)
    mod_slope = -mod_table[:, 1] * frequency * jnp.sin(frequency * time_value)
    return (mod_value, mod_slope)


def attend_group(inputs):
    query, keys, values, query_dot, keys_dot, values_dot = inputs
    scale = 1.0 / math.sqrt(query.shape[-1])
    scores = jnp.einsum("blhe,bmhe->bhlm", query, keys, preferred_element_type=jnp.float32) * scale
    scores_dot = (
        jnp.einsum("blhe,bmhe->bhlm", query_dot, keys, preferred_element_type=jnp.float32)
        + jnp.einsum("blhe,bmhe->bhlm", query, keys_dot, preferred_element_type=jnp.float32)
    ) * scale
    top_score = jnp.max(scores, axis=-1, keepdims=True)
    expo = jnp.exp(scores - top_score)
    probs = expo / jnp.sum(expo, axis=-1, keepdims=True)
    probs_low = probs.astype(jnp.bfloat16)
    output = jnp.einsum("bhlm,bmhe->blhe", probs_low, values, preferred_element_type=jnp.float32)
    row_total = jnp.sum(probs * scores_dot, axis=-1, keepdims=True)
    weighted = probs * (scores_dot - row_total)
    weighted_low = weighted.astype(jnp.bfloat16)
    output_dot = jnp.einsum(
        "bhlm,bmhe->blhe", weighted_low, values, preferred_element_type=jnp.float32
    ) + jnp.einsum("bhlm,bmhe->blhe", probs_low, values_dot, preferred_element_type=jnp.float32)
    return (output, output_dot)


def attend(stacked, group_size):
    batch, length, heads_all, head_size = stacked.shape[2:]
    groups = heads_all // group_size
    shaped = stacked.reshape(2, 3, batch, length, groups, group_size, head_size)
    shaped = jnp.transpose(shaped, (4, 0, 1, 2, 3, 5, 6))
    inputs = (
        shaped[:, 0, 0],
        shaped[:, 0, 1],
        shaped[:, 0, 2],
        shaped[:, 1, 0],
        shaped[:, 1, 1],
        shaped[:, 1, 2],
    )
    output, output_dot = lax.map(attend_group, inputs)
    joined = jnp.stack([output, output_dot], axis=1)
    joined = jnp.transpose(joined, (1, 2, 3, 0, 4, 5))
    return joined.reshape(2, batch, length, heads_all * head_size)


def per_device(stream, spatial_qkv, out_weight, qkv_weight, mod_table, timestep):
    frames_local = stream.shape[1]
    places = stream.shape[2]
    width = stream.shape[3]
    block = lax.all_to_all(spatial_qkv, "pix", split_axis=4, concat_axis=3, tiled=True)
    frames_here = block.shape[2]
    length = block.shape[3]
    channels = block.shape[4]
    shaped = block.reshape(2, 3, frames_here, length, channels // HEAD_DIM, HEAD_DIM)
    attended = attend(shaped, 1).astype(jnp.bfloat16)
    spatial = lax.all_to_all(attended, "pix", split_axis=2, concat_axis=3, tiled=True)
    flat_spatial = spatial.reshape(-1, width)
    projected = jnp.dot(
        flat_spatial,
        lax.all_gather(out_weight, "frame", axis=1, tiled=True),
        preferred_element_type=jnp.float32,
    )
    projected = projected.reshape(2, frames_local, places, width)
    mod_value, mod_slope = modulation(mod_table, timestep)
    primal_in = stream[0].astype(jnp.float32)
    tangent_in = stream[1].astype(jnp.float32)
    hidden = primal_in + mod_value[0] * projected[0]
    hidden_dot = tangent_in + mod_slope[0] * projected[0] + mod_value[0] * projected[1]
    centered = hidden - jnp.mean(hidden, axis=-1, keepdims=True)
    inv_scale = lax.rsqrt(jnp.mean(centered * centered, axis=-1, keepdims=True) + 1e-06)
    normed = centered * inv_scale
    normed_dot = (
        hidden_dot
        - jnp.mean(hidden_dot, axis=-1, keepdims=True)
        - normed * jnp.mean(normed * hidden_dot, axis=-1, keepdims=True)
    ) * inv_scale
    modulated = normed * (1.0 + mod_value[2]) + mod_value[1]
    modulated_dot = normed_dot * (1.0 + mod_value[2]) + normed * mod_slope[2] + mod_slope[1]
    modulated_low = jnp.stack([modulated, modulated_dot]).astype(jnp.bfloat16)
    moved_rows = lax.all_to_all(modulated_low, "frame", split_axis=2, concat_axis=1, tiled=True)
    frames_all = moved_rows.shape[1]
    sub_places = moved_rows.shape[2]
    flat_rows = moved_rows.reshape(-1, width)
    projected_qkv = (
        jnp.dot(
            flat_rows,
            lax.all_gather(qkv_weight, "frame", axis=1, tiled=True),
            preferred_element_type=jnp.float32,
        )
        .astype(jnp.bfloat16)
        .reshape(2, frames_all, sub_places, 3, width)
    )
    moved = jnp.transpose(projected_qkv, (0, 3, 1, 2, 4))
    frames_all = moved.shape[2]
    sub_places = moved.shape[3]
    arranged = jnp.transpose(moved, (0, 1, 3, 2, 4)).reshape(
        2, 3, sub_places, frames_all, width // HEAD_DIM, HEAD_DIM
    )
    attended = attend(arranged, width // HEAD_DIM)
    attended = jnp.transpose(attended, (0, 2, 1, 3))
    temporal = lax.all_to_all(attended, "frame", split_axis=1, concat_axis=2, tiled=True)
    residual = jnp.stack([hidden, hidden_dot])
    return (residual, temporal)


def lane_window(head):
    low = head * HEAD_DIM // LANES * LANES
    high = -(-(head * HEAD_DIM + HEAD_DIM) // LANES) * LANES
    return low, high


def head_mask(head, low, high):
    lane = lax.broadcasted_iota(jnp.int32, (1, high - low), 1) + low
    return (lane >= head * HEAD_DIM) & (lane < (head + 1) * HEAD_DIM)


def across(left, right):
    return lax.dot_general(left, right, (((1,), (1,)), ((), ())), preferred_element_type=jnp.float32)


def attend_head(mask, query, keys, values, query_dot, keys_dot, values_dot, allowed=None):
    scale = 1.0 / math.sqrt(HEAD_DIM)
    keep = mask.astype(jnp.float32).astype(jnp.bfloat16)
    rows = query.shape[0]
    query = query * keep
    query_dot = query_dot * keep
    both = across(jnp.concatenate([query, query_dot], axis=0), keys)
    scores = both[:rows]
    scores_dot = both[rows:] + across(query, keys_dot)
    if allowed is not None:
        scores = jnp.where(allowed, scores, -jnp.inf)
    expo = jnp.exp((scores - jnp.max(scores, axis=-1, keepdims=True)) * scale)
    inverse = 1.0 / jnp.sum(expo, axis=-1, keepdims=True)
    weighted = expo * (scores_dot - inverse * jnp.sum(expo * scores_dot, axis=-1, keepdims=True))
    expo_low = expo.astype(jnp.bfloat16)
    stacked = jnp.concatenate([expo_low, weighted.astype(jnp.bfloat16)], axis=0)
    both = jnp.dot(stacked, values, preferred_element_type=jnp.float32)
    output_dot = both[rows:] * scale + jnp.dot(expo_low, values_dot, preferred_element_type=jnp.float32)
    return both[:rows] * inverse, output_dot * inverse


class LaneTiles:
    def __init__(self, heads):
        self.held = {}
        self.last = {}
        for head in range(heads):
            low, high = lane_window(head)
            for tile in range(low // LANES, high // LANES):
                self.last[tile] = head

    def add(self, head, mask, output, output_dot):
        low, high = lane_window(head)
        done = []
        for tile in range(low // LANES, high // LANES):
            part = slice(tile * LANES - low, (tile + 1) * LANES - low)
            here = mask[:, part]
            pair = (output[:, part], output_dot[:, part])
            if tile in self.held:
                pair = tuple(jnp.where(here, a, b) for a, b in zip(pair, self.held[tile]))
            self.held[tile] = pair
            if self.last[tile] == head:
                done.append((tile, self.held.pop(tile)))
        return done


def fused_kernel(
    n, spatial_in, stream_in, out_own, qkv_own, mod, residual_out, returned,
    spatial, stream, residual, in_sem, peer_kv, out_all, qkv_all, attended, rows_send, rows_recv, qkv, back_send,
    kv_sem, own_sem, up_send, down_send, row_send, grid_recv, core_send, core_recv, x_send, x_recv,
    xcore_send, xcore_recv, row_send_sem, row_recv_sem, back_send_sem, back_recv_sem,
):
    clip, core, me = lax.axis_index("clips"), lax.axis_index("pix"), lax.axis_index("frame")
    side = lax.rem(clip, 2)
    x_peer = clip + 1 - 2 * side
    places, width = stream.shape[2], stream.shape[3]
    part = places // n
    heads = width // HEAD_DIM
    half = n // 2

    depth, row = lax.div(me, 2), lax.rem(me, 2)
    depths = n // 2
    to_peer = {"pix": 1 - core}
    to_x = {"clips": x_peer}
    to_row = {"frame": 2 * depth + 1 - row}

    spatial_copy = pltpu.make_async_copy(spatial_in, spatial, in_sem.at[0])
    stream_copy = pltpu.make_async_copy(stream_in, stream, in_sem.at[1])
    spatial_copy.start()

    barrier = pltpu.get_barrier_semaphore()
    for target in [to_peer, to_x] + [{"frame": lax.rem(me + k, n)} for k in range(1, n)]:
        pl.semaphore_signal(barrier, inc=1, device_id=target, device_id_type=pl.DeviceIdType.MESH)
    pl.semaphore_wait(barrier, n + 1)

    def remote(source, target, send, recv, device):
        return pltpu.make_async_remote_copy(
            src_ref=source, dst_ref=target, send_sem=send, recv_sem=recv,
            device_id=device, device_id_type=pl.DeviceIdType.MESH,
        )

    kv_copy = remote(spatial_in.at[:, 1:3, 0], peer_kv, kv_sem.at[0], kv_sem.at[1], to_peer)
    kv_copy.start()

    gathered = (out_all, qkv_all)
    owned = (out_own, qkv_own)
    sizes = tuple(ref.shape[0] for ref in owned)
    my_third = core + (1 - core) * 2 * side
    peer_third = (1 - core) + core * 2 * side
    x_third = 2 * (1 - side)

    def piece(which, frame, third):
        size = sizes[which] // 3
        return gathered[which].at[pl.ds(pl.multiple_of(frame * sizes[which] + third * size, 16), size)]

    def arrives(block, recv):
        return remote(block, block, kv_sem.at[0], recv, to_peer)

    def moves(which, frame, third, send, recv, device):
        block = piece(which, frame, third)
        return remote(block, block, send.at[which, frame], recv.at[which, frame], device)

    def own_move(which, send, device):
        size = sizes[which] // 3
        source = owned[which].at[pl.ds(pl.multiple_of(my_third * size, 16), size)]
        return remote(
            source, piece(which, me, my_third), send.at[which, me], grid_recv.at[which, me], device
        )

    line_copy = lambda which, frame, sign: moves(
        which, frame, my_third, up_send if sign > 0 else down_send, grid_recv, {"frame": me + 2 * sign}
    )
    row_copy = lambda which, frame: moves(which, frame, my_third, row_send, grid_recv, to_row)
    core_copy = lambda which, frame: moves(which, frame, my_third, core_send, core_recv, to_peer)
    x_copy = lambda which, frame: moves(which, frame, my_third, x_send, x_recv, to_x)
    xcore_copy = lambda which, frame: moves(which, frame, x_third, xcore_send, xcore_recv, to_peer)

    def inside(offset):
        return (depth + offset >= 0) & (depth + offset < depths)

    def when_core(which_core, act):
        pl.when(core == which_core)(act)

    def line_step(which, distance):
        for sign in (1, -1):
            @pl.when(inside(-sign * distance))
            def _():
                frame = me - 2 * sign * distance
                arrives(piece(which, frame, my_third), grid_recv.at[which, frame]).wait_recv()

                @pl.when(inside(sign))
                def _():
                    line_copy(which, frame, sign).start()

                row_copy(which, frame).start()
                when_core(0, lambda: x_copy(which, frame).start())
                core_copy(which, frame).start()

    def offsets(distance):
        return (1, -1) if distance else (1,)

    def row_step(which, distance):
        for sign in offsets(distance):
            @pl.when(inside(sign * distance))
            def _():
                frame = 2 * (depth + sign * distance) + 1 - row
                arrives(piece(which, frame, my_third), grid_recv.at[which, frame]).wait_recv()
                when_core(0, lambda: x_copy(which, frame).start())
                core_copy(which, frame).start()

    def x_step(which, distance, turn):
        for sign in offsets(distance):
            @pl.when(inside(sign * distance) & (core == 0))
            def _():
                frame = 2 * (depth + sign * distance) + (1 - turn) * row + turn * (1 - row)
                arrives(piece(which, frame, x_third), x_recv.at[which, frame]).wait_recv()
                xcore_copy(which, frame).start()

    def all_here(which):
        for k in range(1, n):
            frame = lax.rem(me + k, n)
            arrives(piece(which, frame, peer_third), core_recv.at[which, frame]).wait_recv()
            when_core(
                1, lambda: arrives(piece(which, frame, x_third), xcore_recv.at[which, frame]).wait_recv()
            )

    def all_sent(which):
        own_move(which, row_send, to_row).wait_send()
        for sign in (1, -1):
            @pl.when(inside(sign))
            def _():
                own_move(which, up_send if sign > 0 else down_send, {"frame": me + 2 * sign}).wait_send()

            for distance in range(1, depths):
                @pl.when(inside(-sign * distance))
                def _():
                    frame = me - 2 * sign * distance
                    row_copy(which, frame).wait_send()

                    @pl.when(inside(sign))
                    def _():
                        line_copy(which, frame, sign).wait_send()

        for k in range(1, n):
            frame = lax.rem(me + k, n)
            core_copy(which, frame).wait_send()

            @pl.when(core == 0)
            def _():
                x_copy(which, frame).wait_send()
                xcore_copy(which, frame).wait_send()

    own_copies = []
    for which in (0, 1):
        for sign in (1, -1):
            @pl.when(inside(sign))
            def _():
                own_move(which, up_send if sign > 0 else down_send, {"frame": me + 2 * sign}).start()

        own_move(which, row_send, to_row).start()
        whole = gathered[which].at[pl.ds(pl.multiple_of(me * sizes[which], 16), sizes[which])]
        own_copies.append(pltpu.make_async_copy(owned[which], whole, own_sem.at[which]))
        own_copies[-1].start()
    stream_copy.start()

    events = []
    for distance in range(depths):
        if distance:
            events.append((2 * distance, line_step, (0, distance)))
            events.append((4 * distance + 1, line_step, (1, distance)))
            events.append((14 + distance / 8, x_step, (0, distance, 0)))
            events.append((40 + 2 * distance, x_step, (1, distance, 0)))
        events.append((2 * distance + 2.5, row_step, (0, distance)))
        events.append((4 * distance + 5 if distance < 2 else 30 + distance, row_step, (1, distance)))
        events.append((15 + distance / 8, x_step, (0, distance, 1)))
        events.append((41 + 2 * distance, x_step, (1, distance, 1)))
    events.sort(key=lambda event: event[0])

    def serve(until):
        while events and events[0][0] <= until:
            _, act, args = events.pop(0)
            act(*args)

    def serve_all(which):
        for event in [event for event in events if event[2][0] == which]:
            events.remove(event)
            event[1](*event[2])

    spatial_copy.wait()
    kv_copy.wait_recv()
    tiles = LaneTiles(heads)
    for head in range(heads):
        low, high = lane_window(head)
        mask = head_mask(head, low, high)
        both = lambda t, j: jnp.concatenate([spatial[t, 1 + j, 0, :, low:high], peer_kv[t, j, :, low:high]], axis=0)
        output, output_dot = attend_head(
            mask, spatial[0, 0, 0, :, low:high], both(0, 0), both(0, 1),
            spatial[1, 0, 0, :, low:high], both(1, 0), both(1, 1),
        )
        for tile, pair in tiles.add(head, mask, output, output_dot):
            for t in (0, 1):
                attended[t * places:(t + 1) * places, tile * LANES:(tile + 1) * LANES] = pair[t].astype(jnp.bfloat16)
        serve(head + 1)

    serve_all(0)
    all_here(0)
    own_copies[0].wait()
    stream_copy.wait()

    @pl.loop(0, width // TILE)
    def _(index):
        columns = pl.ds(pl.multiple_of(index * TILE, TILE), TILE)
        projected = across(attended[...], out_all[columns, :])
        gate, gate_slope = mod[0:1, columns], mod[3:4, columns]
        residual[0, 0, :, columns] = stream[0, 0, :, columns].astype(jnp.float32) + gate * projected[:places]
        residual[1, 0, :, columns] = (
            stream[1, 0, :, columns].astype(jnp.float32)
            + gate_slope * projected[:places]
            + gate * projected[places:]
        )

    serve(17)
    row_copies = []
    for k in list(range(1, n)) + [0]:
        frame = lax.rem(me + k, n)
        rows = pl.ds(pl.multiple_of(frame * part, 8), part)
        hidden, hidden_dot = residual[0, 0, rows, :], residual[1, 0, rows, :]
        centered = hidden - jnp.mean(hidden, axis=-1, keepdims=True)
        inv_scale = lax.rsqrt(jnp.mean(centered * centered, axis=-1, keepdims=True) + 1e-06)
        normed = centered * inv_scale
        normed_dot = (
            hidden_dot
            - jnp.mean(hidden_dot, axis=-1, keepdims=True)
            - normed * jnp.mean(normed * hidden_dot, axis=-1, keepdims=True)
        ) * inv_scale
        modulated = normed * (1.0 + mod[2:3, :]) + mod[1:2, :]
        modulated_dot = normed_dot * (1.0 + mod[2:3, :]) + normed * mod[5:6, :] + mod[4:5, :]
        block = jnp.concatenate([modulated, modulated_dot], axis=0).astype(jnp.bfloat16)
        mine = pl.ds(pl.multiple_of(me * 2 * part, 16), 2 * part)
        if k == 0:
            rows_recv[mine, :] = block
        else:
            theirs = pl.ds(pl.multiple_of(frame * 2 * part, 16), 2 * part)
            rows_send[theirs, :] = block
            row_copies.append(remote(
                rows_send.at[theirs], rows_recv.at[mine], row_send_sem.at[k], row_recv_sem.at[k], {"frame": frame}
            ))
            row_copies[-1].start()
        serve(18 + k)

    residual_copy = pltpu.make_async_copy(residual, residual_out, in_sem.at[2])
    residual_copy.start()
    serve_all(1)
    all_here(1)
    own_copies[1].wait()
    for k in range(1, n):
        source = lax.rem(me - k + n, n)
        arrives(rows_recv.at[pl.ds(pl.multiple_of(source * 2 * part, 16), 2 * part)], row_recv_sem.at[k]).wait_recv()

    def project_chunk(chunk):
        @pl.loop(0, 3)
        def _(index):
            columns = pl.ds(pl.multiple_of(index * width + chunk * TILE, LANES), TILE)
            product = across(rows_recv[...], qkv_all[columns, :])
            for t in (0, 1):
                kept = [product[(2 * f + t) * part:(2 * f + t + 1) * part] for f in range(n)]
                qkv[t, :, columns] = jnp.concatenate(kept, axis=0).astype(jnp.bfloat16)

    rows = n * part
    one = lax.rem(lax.broadcasted_iota(jnp.int32, (rows, rows), 0), part)
    two = lax.rem(lax.broadcasted_iota(jnp.int32, (rows, rows), 1), part)
    allowed = one == two
    tiles = LaneTiles(heads)
    chunks = back_send.shape[0]
    chunk_tiles = width // LANES // chunks
    back_copies = []
    pieces = {}
    ready = 0
    for head in range(heads):
        low, high = lane_window(head)
        while ready * TILE < high:
            project_chunk(ready)
            ready += 1
        mask = head_mask(head, low, high)
        take = lambda t, j: qkv[t, :, j * width + low:j * width + high]
        output, output_dot = attend_head(
            mask, take(0, 0), take(0, 1), take(0, 2), take(1, 0), take(1, 1), take(1, 2), allowed
        )
        for tile, pair in tiles.add(head, mask, output, output_dot):
            chunk, inner = tile // chunk_tiles, tile % chunk_tiles
            for f in range(n):
                block = jnp.concatenate([value[f * part:(f + 1) * part] for value in pair], axis=0)
                back_send[chunk, f, :, inner * LANES:(inner + 1) * LANES] = block.astype(jnp.bfloat16)
            if inner == chunk_tiles - 1:
                own = pltpu.make_async_copy(
                    back_send.at[chunk, me], returned.at[chunk, me], back_send_sem.at[chunk, 0]
                )
                own.start()
                back_copies.append(own)
                for k in range(1, n):
                    frame = lax.rem(me + k, n)
                    copy = remote(
                        back_send.at[chunk, frame], returned.at[chunk, me],
                        back_send_sem.at[chunk, k], back_recv_sem.at[chunk, k], {"frame": frame},
                    )
                    copy.start()
                    pieces[chunk, k] = copy

    residual_copy.wait()
    kv_copy.wait_send()
    for which in (0, 1):
        all_sent(which)
    for copy in row_copies:
        copy.wait_send()
    for copy in back_copies:
        copy.wait()
    for (chunk, k), copy in pieces.items():
        copy.wait_send()
        source = lax.rem(me - k + n, n)
        arrives(returned.at[chunk, source], back_recv_sem.at[chunk, k]).wait_recv()


def finish_kernel(residual, returned, residual_out, temporal_out, blocks, held, temporal, sem):
    chunks, n, rows, tile = returned.shape
    part = rows // 2
    arrivals = [pltpu.make_async_copy(returned.at[c], blocks.at[c], sem.at[c]) for c in range(chunks)]
    passing = [pltpu.make_async_copy(residual.at[t], held.at[t], sem.at[2 * chunks + t]) for t in (0, 1)]
    for copy in arrivals + passing:
        copy.start()
    leaving = []
    for chunk in range(chunks):
        arrivals[chunk].wait()
        for f in range(n):
            block = blocks[chunk, f].astype(jnp.float32)
            for t in (0, 1):
                temporal[t, 0, f * part:(f + 1) * part, chunk * tile:(chunk + 1) * tile] = (
                    block[t * part:(t + 1) * part]
                )
        columns = pl.ds(chunk * tile, tile)
        leaving.append(pltpu.make_async_copy(
            temporal.at[:, :, :, columns], temporal_out.at[:, :, :, columns], sem.at[chunks + chunk]
        ))
        leaving[-1].start()
        if chunk < 2:
            passing[chunk].wait()
            leaving.append(pltpu.make_async_copy(
                held.at[chunk], residual_out.at[chunk], sem.at[2 * chunks + 2 + chunk]
            ))
            leaving[-1].start()
    for copy in leaving:
        copy.wait()


def per_device_fused(n, stream, spatial_qkv, out_weight, qkv_weight, mod_table, timestep):
    places, width = stream.shape[2], stream.shape[3]
    part = places // n
    chunks = width // TILE
    mod = jnp.concatenate(modulation(mod_table, timestep), axis=0)
    bf16, f32 = jnp.bfloat16, jnp.float32
    dma = pltpu.SemaphoreType.DMA
    vmem = pl.BlockSpec(memory_space=pltpu.VMEM)
    anywhere = pl.BlockSpec(memory_space=pl.ANY)
    residual, returned = pl.pallas_call(
        functools.partial(fused_kernel, n),
        out_shape=(
            jax.ShapeDtypeStruct(stream.shape, f32),
            jax.ShapeDtypeStruct((chunks, n, 2 * part, TILE), bf16),
        ),
        in_specs=[anywhere] * 4 + [vmem],
        out_specs=(anywhere, vmem),
        scratch_shapes=[
            pltpu.VMEM(spatial_qkv.shape, bf16),
            pltpu.VMEM(stream.shape, bf16),
            pltpu.VMEM(stream.shape, f32),
            dma((3,)),
            pltpu.VMEM((2, 2, places, width), bf16),
            pltpu.VMEM((width, width), bf16),
            pltpu.VMEM((3 * width, width), bf16),
            pltpu.VMEM((2 * places, width), bf16),
            pltpu.VMEM((2 * places, width), bf16),
            pltpu.VMEM((2 * places, width), bf16),
            pltpu.VMEM((2, places, 3 * width), bf16),
            pltpu.VMEM((chunks, n, 2 * part, TILE), bf16),
            dma((2,)), dma((2,)),
        ] + [dma((2, n))] * 10 + [dma((n,))] * 2 + [dma((chunks, n))] * 2,
        compiler_params=pltpu.CompilerParams(
            collective_id=0, has_side_effects=True, vmem_limit_bytes=56 * 1024 * 1024
        ),
    )(spatial_qkv, stream, out_weight.T, qkv_weight.T, mod)
    return tuple(pl.pallas_call(
        finish_kernel,
        out_shape=(jax.ShapeDtypeStruct(stream.shape, f32),) * 2,
        in_specs=[anywhere] * 2,
        out_specs=(anywhere,) * 2,
        scratch_shapes=[
            pltpu.VMEM((chunks, n, 2 * part, TILE), bf16),
            pltpu.VMEM(stream.shape, f32),
            pltpu.VMEM(stream.shape, f32),
            dma((2 * chunks + 4,)),
        ],
        compiler_params=pltpu.CompilerParams(vmem_limit_bytes=56 * 1024 * 1024),
    )(residual, returned))


def fits_fused(mesh, places, width, out_columns, qkv_columns, frames_local):
    n = mesh.shape["frame"]
    return (
        mesh.shape["pix"] == 2
        and mesh.shape["clips"] % 2 == 0
        and n % 2 == 0
        and frames_local == 1
        and places % n == 0
        and (places // n) % 8 == 0
        and places % 16 == 0
        and width % TILE == 0
        and width >= 2 * TILE
        and width % HEAD_DIM == 0
        and out_columns % 48 == 0
        and qkv_columns % 48 == 0
    )


def solution(mesh):
    in_specs = (
        P(None, ("clips", "frame"), "pix", None),
        P(None, None, ("clips", "frame"), "pix", None),
        P(None, "frame"),
        P(None, "frame"),
        P(),
        P("clips"),
    )
    out_specs = (P(None, ("clips", "frame"), "pix", None), P(None, ("clips", "frame"), "pix", None))

    def local(stream, spatial_qkv, out_weight, qkv_weight, mod_table, timestep):
        args = (stream, spatial_qkv, out_weight, qkv_weight, mod_table, timestep)
        if fits_fused(
            mesh, stream.shape[2], stream.shape[3], out_weight.shape[1], qkv_weight.shape[1], stream.shape[1]
        ):
            return per_device_fused(mesh.shape["frame"], *args)
        return per_device(*args)

    return jax.shard_map(local, mesh=mesh, in_specs=in_specs, out_specs=out_specs, check_vma=False)
```

```python
import functools
import math

import jax
import jax.numpy as jnp
from jax import lax
from jax.experimental import pallas as pl
from jax.experimental.pallas import tpu as pltpu
from jax.sharding import PartitionSpec as P

HEAD_DIM = 72
LANES = 128
TILE = 384


def modulation(mod_table, timestep):
    width = mod_table.shape[-1]
    frequency = jnp.exp(-math.log(10.0) * jnp.arange(width).astype(jnp.float32) / width)
    time_value = timestep[0].astype(jnp.float32) * (math.pi / 1000.0)
    mod_value = mod_table[:, 0] + mod_table[:, 1] * jnp.cos(frequency * time_value)
    mod_slope = -mod_table[:, 1] * frequency * jnp.sin(frequency * time_value)
    return (mod_value, mod_slope)


def attend_group(inputs):
    query, keys, values, query_dot, keys_dot, values_dot = inputs
    scale = 1.0 / math.sqrt(query.shape[-1])
    scores = jnp.einsum("blhe,bmhe->bhlm", query, keys, preferred_element_type=jnp.float32) * scale
    scores_dot = (
        jnp.einsum("blhe,bmhe->bhlm", query_dot, keys, preferred_element_type=jnp.float32)
        + jnp.einsum("blhe,bmhe->bhlm", query, keys_dot, preferred_element_type=jnp.float32)
    ) * scale
    top_score = jnp.max(scores, axis=-1, keepdims=True)
    expo = jnp.exp(scores - top_score)
    probs = expo / jnp.sum(expo, axis=-1, keepdims=True)
    probs_low = probs.astype(jnp.bfloat16)
    output = jnp.einsum("bhlm,bmhe->blhe", probs_low, values, preferred_element_type=jnp.float32)
    row_total = jnp.sum(probs * scores_dot, axis=-1, keepdims=True)
    weighted = probs * (scores_dot - row_total)
    weighted_low = weighted.astype(jnp.bfloat16)
    output_dot = jnp.einsum(
        "bhlm,bmhe->blhe", weighted_low, values, preferred_element_type=jnp.float32
    ) + jnp.einsum("bhlm,bmhe->blhe", probs_low, values_dot, preferred_element_type=jnp.float32)
    return (output, output_dot)


def attend(stacked, group_size):
    batch, length, heads_all, head_size = stacked.shape[2:]
    groups = heads_all // group_size
    shaped = stacked.reshape(2, 3, batch, length, groups, group_size, head_size)
    shaped = jnp.transpose(shaped, (4, 0, 1, 2, 3, 5, 6))
    inputs = (
        shaped[:, 0, 0],
        shaped[:, 0, 1],
        shaped[:, 0, 2],
        shaped[:, 1, 0],
        shaped[:, 1, 1],
        shaped[:, 1, 2],
    )
    output, output_dot = lax.map(attend_group, inputs)
    joined = jnp.stack([output, output_dot], axis=1)
    joined = jnp.transpose(joined, (1, 2, 3, 0, 4, 5))
    return joined.reshape(2, batch, length, heads_all * head_size)


def per_device(stream, spatial_qkv, out_weight, qkv_weight, mod_table, timestep):
    frames_local = stream.shape[1]
    places = stream.shape[2]
    width = stream.shape[3]
    block = lax.all_to_all(spatial_qkv, "pix", split_axis=4, concat_axis=3, tiled=True)
    frames_here = block.shape[2]
    length = block.shape[3]
    channels = block.shape[4]
    shaped = block.reshape(2, 3, frames_here, length, channels // HEAD_DIM, HEAD_DIM)
    attended = attend(shaped, 1).astype(jnp.bfloat16)
    spatial = lax.all_to_all(attended, "pix", split_axis=2, concat_axis=3, tiled=True)
    flat_spatial = spatial.reshape(-1, width)
    projected = jnp.dot(
        flat_spatial,
        lax.all_gather(out_weight, "frame", axis=1, tiled=True),
        preferred_element_type=jnp.float32,
    )
    projected = projected.reshape(2, frames_local, places, width)
    mod_value, mod_slope = modulation(mod_table, timestep)
    primal_in = stream[0].astype(jnp.float32)
    tangent_in = stream[1].astype(jnp.float32)
    hidden = primal_in + mod_value[0] * projected[0]
    hidden_dot = tangent_in + mod_slope[0] * projected[0] + mod_value[0] * projected[1]
    centered = hidden - jnp.mean(hidden, axis=-1, keepdims=True)
    inv_scale = lax.rsqrt(jnp.mean(centered * centered, axis=-1, keepdims=True) + 1e-06)
    normed = centered * inv_scale
    normed_dot = (
        hidden_dot
        - jnp.mean(hidden_dot, axis=-1, keepdims=True)
        - normed * jnp.mean(normed * hidden_dot, axis=-1, keepdims=True)
    ) * inv_scale
    modulated = normed * (1.0 + mod_value[2]) + mod_value[1]
    modulated_dot = normed_dot * (1.0 + mod_value[2]) + normed * mod_slope[2] + mod_slope[1]
    modulated_low = jnp.stack([modulated, modulated_dot]).astype(jnp.bfloat16)
    moved_rows = lax.all_to_all(modulated_low, "frame", split_axis=2, concat_axis=1, tiled=True)
    frames_all = moved_rows.shape[1]
    sub_places = moved_rows.shape[2]
    flat_rows = moved_rows.reshape(-1, width)
    projected_qkv = (
        jnp.dot(
            flat_rows,
            lax.all_gather(qkv_weight, "frame", axis=1, tiled=True),
            preferred_element_type=jnp.float32,
        )
        .astype(jnp.bfloat16)
        .reshape(2, frames_all, sub_places, 3, width)
    )
    moved = jnp.transpose(projected_qkv, (0, 3, 1, 2, 4))
    frames_all = moved.shape[2]
    sub_places = moved.shape[3]
    arranged = jnp.transpose(moved, (0, 1, 3, 2, 4)).reshape(
        2, 3, sub_places, frames_all, width // HEAD_DIM, HEAD_DIM
    )
    attended = attend(arranged, width // HEAD_DIM)
    attended = jnp.transpose(attended, (0, 2, 1, 3))
    temporal = lax.all_to_all(attended, "frame", split_axis=1, concat_axis=2, tiled=True)
    residual = jnp.stack([hidden, hidden_dot])
    return (residual, temporal)


def lane_window(head):
    low = head * HEAD_DIM // LANES * LANES
    high = -(-(head * HEAD_DIM + HEAD_DIM) // LANES) * LANES
    return low, high


def head_mask(head, low, high):
    lane = lax.broadcasted_iota(jnp.int32, (1, high - low), 1) + low
    return (lane >= head * HEAD_DIM) & (lane < (head + 1) * HEAD_DIM)


def across(left, right):
    return lax.dot_general(left, right, (((1,), (1,)), ((), ())), preferred_element_type=jnp.float32)


def attend_head(mask, query, keys, values, query_dot, keys_dot, values_dot, allowed=None):
    scale = 1.0 / math.sqrt(HEAD_DIM)
    keep = mask.astype(jnp.float32).astype(jnp.bfloat16)
    rows = query.shape[0]
    query = query * keep
    query_dot = query_dot * keep
    both = across(jnp.concatenate([query, query_dot], axis=0), keys)
    scores = both[:rows]
    scores_dot = both[rows:] + across(query, keys_dot)
    if allowed is not None:
        scores = jnp.where(allowed, scores, -jnp.inf)
    expo = jnp.exp((scores - jnp.max(scores, axis=-1, keepdims=True)) * scale)
    inverse = 1.0 / jnp.sum(expo, axis=-1, keepdims=True)
    weighted = expo * (scores_dot - inverse * jnp.sum(expo * scores_dot, axis=-1, keepdims=True))
    expo_low = expo.astype(jnp.bfloat16)
    stacked = jnp.concatenate([expo_low, weighted.astype(jnp.bfloat16)], axis=0)
    both = jnp.dot(stacked, values, preferred_element_type=jnp.float32)
    output_dot = both[rows:] * scale + jnp.dot(expo_low, values_dot, preferred_element_type=jnp.float32)
    return both[:rows] * inverse, output_dot * inverse


class LaneTiles:
    def __init__(self, heads):
        self.held = {}
        self.last = {}
        for head in range(heads):
            low, high = lane_window(head)
            for tile in range(low // LANES, high // LANES):
                self.last[tile] = head

    def add(self, head, mask, output, output_dot):
        low, high = lane_window(head)
        done = []
        for tile in range(low // LANES, high // LANES):
            part = slice(tile * LANES - low, (tile + 1) * LANES - low)
            here = mask[:, part]
            pair = (output[:, part], output_dot[:, part])
            if tile in self.held:
                pair = tuple(jnp.where(here, a, b) for a, b in zip(pair, self.held[tile]))
            self.held[tile] = pair
            if self.last[tile] == head:
                done.append((tile, self.held.pop(tile)))
        return done


def fused_kernel(
    n, spatial_in, stream_in, out_own, qkv_own, mod, residual_out, returned,
    spatial, stream, residual, in_sem, peer_kv, out_all, qkv_all, attended, rows_send, rows_recv, qkv, back_send,
    kv_sem, own_sem, up_send, down_send, row_send, grid_recv, core_send, core_recv, x_send, x_recv,
    xcore_send, xcore_recv, row_send_sem, row_recv_sem, back_send_sem, back_recv_sem,
):
    clip, core, me = lax.axis_index("clips"), lax.axis_index("pix"), lax.axis_index("frame")
    side = lax.rem(clip, 2)
    x_peer = clip + 1 - 2 * side
    places, width = stream.shape[2], stream.shape[3]
    part = places // n
    heads = width // HEAD_DIM
    half = n // 2

    depth, row = lax.div(me, 2), lax.rem(me, 2)
    depths = n // 2
    to_peer = {"pix": 1 - core}
    to_x = {"clips": x_peer}
    to_row = {"frame": 2 * depth + 1 - row}

    spatial_copy = pltpu.make_async_copy(spatial_in, spatial, in_sem.at[0])
    stream_copy = pltpu.make_async_copy(stream_in, stream, in_sem.at[1])
    spatial_copy.start()

    barrier = pltpu.get_barrier_semaphore()
    for target in [to_peer, to_x] + [{"frame": lax.rem(me + k, n)} for k in range(1, n)]:
        pl.semaphore_signal(barrier, inc=1, device_id=target, device_id_type=pl.DeviceIdType.MESH)
    pl.semaphore_wait(barrier, n + 1)

    def remote(source, target, send, recv, device):
        return pltpu.make_async_remote_copy(
            src_ref=source, dst_ref=target, send_sem=send, recv_sem=recv,
            device_id=device, device_id_type=pl.DeviceIdType.MESH,
        )

    kv_copy = remote(spatial_in.at[:, 1:3, 0], peer_kv, kv_sem.at[0], kv_sem.at[1], to_peer)
    kv_copy.start()

    gathered = (out_all, qkv_all)
    owned = (out_own, qkv_own)
    sizes = tuple(ref.shape[0] for ref in owned)
    my_third = core + (1 - core) * 2 * side
    peer_third = (1 - core) + core * 2 * side
    x_third = 2 * (1 - side)

    def piece(which, frame, third):
        size = sizes[which] // 3
        return gathered[which].at[pl.ds(pl.multiple_of(frame * sizes[which] + third * size, 16), size)]

    def arrives(block, recv):
        return remote(block, block, kv_sem.at[0], recv, to_peer)

    def moves(which, frame, third, send, recv, device):
        block = piece(which, frame, third)
        return remote(block, block, send.at[which, frame], recv.at[which, frame], device)

    def own_move(which, send, device):
        size = sizes[which] // 3
        source = owned[which].at[pl.ds(pl.multiple_of(my_third * size, 16), size)]
        return remote(
            source, piece(which, me, my_third), send.at[which, me], grid_recv.at[which, me], device
        )

    line_copy = lambda which, frame, sign: moves(
        which, frame, my_third, up_send if sign > 0 else down_send, grid_recv, {"frame": me + 2 * sign}
    )
    row_copy = lambda which, frame: moves(which, frame, my_third, row_send, grid_recv, to_row)
    core_copy = lambda which, frame: moves(which, frame, my_third, core_send, core_recv, to_peer)
    x_copy = lambda which, frame: moves(which, frame, my_third, x_send, x_recv, to_x)
    xcore_copy = lambda which, frame: moves(which, frame, x_third, xcore_send, xcore_recv, to_peer)

    def inside(offset):
        return (depth + offset >= 0) & (depth + offset < depths)

    def when_core(which_core, act):
        pl.when(core == which_core)(act)

    def line_step(which, distance):
        for sign in (1, -1):
            @pl.when(inside(-sign * distance))
            def _():
                frame = me - 2 * sign * distance
                arrives(piece(which, frame, my_third), grid_recv.at[which, frame]).wait_recv()

                @pl.when(inside(sign))
                def _():
                    line_copy(which, frame, sign).start()

                row_copy(which, frame).start()
                when_core(0, lambda: x_copy(which, frame).start())
                core_copy(which, frame).start()

    def offsets(distance):
        return (1, -1) if distance else (1,)

    def row_step(which, distance):
        for sign in offsets(distance):
            @pl.when(inside(sign * distance))
            def _():
                frame = 2 * (depth + sign * distance) + 1 - row
                arrives(piece(which, frame, my_third), grid_recv.at[which, frame]).wait_recv()
                when_core(0, lambda: x_copy(which, frame).start())
                core_copy(which, frame).start()

    def x_step(which, distance, turn):
        for sign in offsets(distance):
            @pl.when(inside(sign * distance) & (core == 0))
            def _():
                frame = 2 * (depth + sign * distance) + (1 - turn) * row + turn * (1 - row)
                arrives(piece(which, frame, x_third), x_recv.at[which, frame]).wait_recv()
                xcore_copy(which, frame).start()

    def all_here(which):
        for k in range(1, n):
            frame = lax.rem(me + k, n)
            arrives(piece(which, frame, peer_third), core_recv.at[which, frame]).wait_recv()
            when_core(
                1, lambda: arrives(piece(which, frame, x_third), xcore_recv.at[which, frame]).wait_recv()
            )

    def all_sent(which):
        own_move(which, row_send, to_row).wait_send()
        for sign in (1, -1):
            @pl.when(inside(sign))
            def _():
                own_move(which, up_send if sign > 0 else down_send, {"frame": me + 2 * sign}).wait_send()

            for distance in range(1, depths):
                @pl.when(inside(-sign * distance))
                def _():
                    frame = me - 2 * sign * distance
                    row_copy(which, frame).wait_send()

                    @pl.when(inside(sign))
                    def _():
                        line_copy(which, frame, sign).wait_send()

        for k in range(1, n):
            frame = lax.rem(me + k, n)
            core_copy(which, frame).wait_send()

            @pl.when(core == 0)
            def _():
                x_copy(which, frame).wait_send()
                xcore_copy(which, frame).wait_send()

    own_copies = []
    for which in (0, 1):
        for sign in (1, -1):
            @pl.when(inside(sign))
            def _():
                own_move(which, up_send if sign > 0 else down_send, {"frame": me + 2 * sign}).start()

        own_move(which, row_send, to_row).start()
        whole = gathered[which].at[pl.ds(pl.multiple_of(me * sizes[which], 16), sizes[which])]
        own_copies.append(pltpu.make_async_copy(owned[which], whole, own_sem.at[which]))
        own_copies[-1].start()
    stream_copy.start()

    events = []
    for distance in range(depths):
        if distance:
            events.append((2 * distance, line_step, (0, distance)))
            events.append((4 * distance + 1, line_step, (1, distance)))
            events.append((14 + distance / 8, x_step, (0, distance, 0)))
            events.append((40 + 2 * distance, x_step, (1, distance, 0)))
        events.append((2 * distance + 2.5, row_step, (0, distance)))
        events.append((4 * distance + 5, row_step, (1, distance)))
        events.append((15 + distance / 8, x_step, (0, distance, 1)))
        events.append((41 + 2 * distance, x_step, (1, distance, 1)))
    events.sort(key=lambda event: event[0])

    def serve(until):
        while events and events[0][0] <= until:
            _, act, args = events.pop(0)
            act(*args)

    def serve_all(which):
        for event in [event for event in events if event[2][0] == which]:
            events.remove(event)
            event[1](*event[2])

    spatial_copy.wait()
    kv_copy.wait_recv()
    tiles = LaneTiles(heads)
    for head in range(heads):
        low, high = lane_window(head)
        mask = head_mask(head, low, high)
        both = lambda t, j: jnp.concatenate([spatial[t, 1 + j, 0, :, low:high], peer_kv[t, j, :, low:high]], axis=0)
        output, output_dot = attend_head(
            mask, spatial[0, 0, 0, :, low:high], both(0, 0), both(0, 1),
            spatial[1, 0, 0, :, low:high], both(1, 0), both(1, 1),
        )
        for tile, pair in tiles.add(head, mask, output, output_dot):
            for t in (0, 1):
                attended[t * places:(t + 1) * places, tile * LANES:(tile + 1) * LANES] = pair[t].astype(jnp.bfloat16)
        serve(head + 1)

    serve_all(0)
    all_here(0)
    own_copies[0].wait()
    stream_copy.wait()

    @pl.loop(0, width // TILE)
    def _(index):
        columns = pl.ds(pl.multiple_of(index * TILE, TILE), TILE)
        projected = across(attended[...], out_all[columns, :])
        gate, gate_slope = mod[0:1, columns], mod[3:4, columns]
        residual[0, 0, :, columns] = stream[0, 0, :, columns].astype(jnp.float32) + gate * projected[:places]
        residual[1, 0, :, columns] = (
            stream[1, 0, :, columns].astype(jnp.float32)
            + gate_slope * projected[:places]
            + gate * projected[places:]
        )

    serve(17)
    row_copies = []
    for k in list(range(1, n)) + [0]:
        frame = lax.rem(me + k, n)
        rows = pl.ds(pl.multiple_of(frame * part, 8), part)
        hidden, hidden_dot = residual[0, 0, rows, :], residual[1, 0, rows, :]
        centered = hidden - jnp.mean(hidden, axis=-1, keepdims=True)
        inv_scale = lax.rsqrt(jnp.mean(centered * centered, axis=-1, keepdims=True) + 1e-06)
        normed = centered * inv_scale
        normed_dot = (
            hidden_dot
            - jnp.mean(hidden_dot, axis=-1, keepdims=True)
            - normed * jnp.mean(normed * hidden_dot, axis=-1, keepdims=True)
        ) * inv_scale
        modulated = normed * (1.0 + mod[2:3, :]) + mod[1:2, :]
        modulated_dot = normed_dot * (1.0 + mod[2:3, :]) + normed * mod[5:6, :] + mod[4:5, :]
        block = jnp.concatenate([modulated, modulated_dot], axis=0).astype(jnp.bfloat16)
        mine = pl.ds(pl.multiple_of(me * 2 * part, 16), 2 * part)
        if k == 0:
            rows_recv[mine, :] = block
        else:
            theirs = pl.ds(pl.multiple_of(frame * 2 * part, 16), 2 * part)
            rows_send[theirs, :] = block
            row_copies.append(remote(
                rows_send.at[theirs], rows_recv.at[mine], row_send_sem.at[k], row_recv_sem.at[k], {"frame": frame}
            ))
            row_copies[-1].start()
        serve(18 + k)

    residual_copy = pltpu.make_async_copy(residual, residual_out, in_sem.at[2])
    residual_copy.start()
    serve_all(1)
    all_here(1)
    own_copies[1].wait()
    for k in range(1, n):
        source = lax.rem(me - k + n, n)
        arrives(rows_recv.at[pl.ds(pl.multiple_of(source * 2 * part, 16), 2 * part)], row_recv_sem.at[k]).wait_recv()

    def project_chunk(chunk):
        @pl.loop(0, 3)
        def _(index):
            columns = pl.ds(pl.multiple_of(index * width + chunk * TILE, LANES), TILE)
            product = across(rows_recv[...], qkv_all[columns, :])
            for t in (0, 1):
                kept = [product[(2 * f + t) * part:(2 * f + t + 1) * part] for f in range(n)]
                qkv[t, :, columns] = jnp.concatenate(kept, axis=0).astype(jnp.bfloat16)

    rows = n * part
    one = lax.rem(lax.broadcasted_iota(jnp.int32, (rows, rows), 0), part)
    two = lax.rem(lax.broadcasted_iota(jnp.int32, (rows, rows), 1), part)
    allowed = one == two
    tiles = LaneTiles(heads)
    chunks = back_send.shape[0]
    chunk_tiles = width // LANES // chunks
    back_copies = []
    pieces = {}
    ready = 0
    for head in range(heads):
        low, high = lane_window(head)
        while ready * TILE < high:
            project_chunk(ready)
            ready += 1
        mask = head_mask(head, low, high)
        take = lambda t, j: qkv[t, :, j * width + low:j * width + high]
        output, output_dot = attend_head(
            mask, take(0, 0), take(0, 1), take(0, 2), take(1, 0), take(1, 1), take(1, 2), allowed
        )
        for tile, pair in tiles.add(head, mask, output, output_dot):
            chunk, inner = tile // chunk_tiles, tile % chunk_tiles
            for f in range(n):
                block = jnp.concatenate([value[f * part:(f + 1) * part] for value in pair], axis=0)
                back_send[chunk, f, :, inner * LANES:(inner + 1) * LANES] = block.astype(jnp.bfloat16)
            if inner == chunk_tiles - 1:
                own = pltpu.make_async_copy(
                    back_send.at[chunk, me], returned.at[chunk, me], back_send_sem.at[chunk, 0]
                )
                own.start()
                back_copies.append(own)
                for k in range(1, n):
                    frame = lax.rem(me + k, n)
                    copy = remote(
                        back_send.at[chunk, frame], returned.at[chunk, me],
                        back_send_sem.at[chunk, k], back_recv_sem.at[chunk, k], {"frame": frame},
                    )
                    copy.start()
                    pieces[chunk, k] = copy

    residual_copy.wait()
    kv_copy.wait_send()
    for which in (0, 1):
        all_sent(which)
    for copy in row_copies:
        copy.wait_send()
    for copy in back_copies:
        copy.wait()
    for (chunk, k), copy in pieces.items():
        copy.wait_send()
        source = lax.rem(me - k + n, n)
        arrives(returned.at[chunk, source], back_recv_sem.at[chunk, k]).wait_recv()


def finish_kernel(residual, returned, residual_out, temporal_out, blocks, held, temporal, sem):
    chunks, n, rows, tile = returned.shape
    part = rows // 2
    arrivals = [pltpu.make_async_copy(returned.at[c], blocks.at[c], sem.at[c]) for c in range(chunks)]
    passing = [pltpu.make_async_copy(residual.at[t], held.at[t], sem.at[2 * chunks + t]) for t in (0, 1)]
    for copy in arrivals + passing:
        copy.start()
    leaving = []
    for chunk in range(chunks):
        arrivals[chunk].wait()
        for f in range(n):
            block = blocks[chunk, f].astype(jnp.float32)
            for t in (0, 1):
                temporal[t, 0, f * part:(f + 1) * part, chunk * tile:(chunk + 1) * tile] = (
                    block[t * part:(t + 1) * part]
                )
        columns = pl.ds(chunk * tile, tile)
        leaving.append(pltpu.make_async_copy(
            temporal.at[:, :, :, columns], temporal_out.at[:, :, :, columns], sem.at[chunks + chunk]
        ))
        leaving[-1].start()
        if chunk < 2:
            passing[chunk].wait()
            leaving.append(pltpu.make_async_copy(
                held.at[chunk], residual_out.at[chunk], sem.at[2 * chunks + 2 + chunk]
            ))
            leaving[-1].start()
    for copy in leaving:
        copy.wait()


def per_device_fused(n, stream, spatial_qkv, out_weight, qkv_weight, mod_table, timestep):
    places, width = stream.shape[2], stream.shape[3]
    part = places // n
    chunks = width // TILE
    mod = jnp.concatenate(modulation(mod_table, timestep), axis=0)
    bf16, f32 = jnp.bfloat16, jnp.float32
    dma = pltpu.SemaphoreType.DMA
    vmem = pl.BlockSpec(memory_space=pltpu.VMEM)
    anywhere = pl.BlockSpec(memory_space=pl.ANY)
    residual, returned = pl.pallas_call(
        functools.partial(fused_kernel, n),
        out_shape=(
            jax.ShapeDtypeStruct(stream.shape, f32),
            jax.ShapeDtypeStruct((chunks, n, 2 * part, TILE), bf16),
        ),
        in_specs=[anywhere] * 4 + [vmem],
        out_specs=(anywhere, vmem),
        scratch_shapes=[
            pltpu.VMEM(spatial_qkv.shape, bf16),
            pltpu.VMEM(stream.shape, bf16),
            pltpu.VMEM(stream.shape, f32),
            dma((3,)),
            pltpu.VMEM((2, 2, places, width), bf16),
            pltpu.VMEM((width, width), bf16),
            pltpu.VMEM((3 * width, width), bf16),
            pltpu.VMEM((2 * places, width), bf16),
            pltpu.VMEM((2 * places, width), bf16),
            pltpu.VMEM((2 * places, width), bf16),
            pltpu.VMEM((2, places, 3 * width), bf16),
            pltpu.VMEM((chunks, n, 2 * part, TILE), bf16),
            dma((2,)), dma((2,)),
        ] + [dma((2, n))] * 10 + [dma((n,))] * 2 + [dma((chunks, n))] * 2,
        compiler_params=pltpu.CompilerParams(
            collective_id=0, has_side_effects=True, vmem_limit_bytes=56 * 1024 * 1024
        ),
    )(spatial_qkv, stream, out_weight.T, qkv_weight.T, mod)
    return tuple(pl.pallas_call(
        finish_kernel,
        out_shape=(jax.ShapeDtypeStruct(stream.shape, f32),) * 2,
        in_specs=[anywhere] * 2,
        out_specs=(anywhere,) * 2,
        scratch_shapes=[
            pltpu.VMEM((chunks, n, 2 * part, TILE), bf16),
            pltpu.VMEM(stream.shape, f32),
            pltpu.VMEM(stream.shape, f32),
            dma((2 * chunks + 4,)),
        ],
        compiler_params=pltpu.CompilerParams(vmem_limit_bytes=56 * 1024 * 1024),
    )(residual, returned))


def fits_fused(mesh, places, width, out_columns, qkv_columns, frames_local):
    n = mesh.shape["frame"]
    return (
        mesh.shape["pix"] == 2
        and mesh.shape["clips"] % 2 == 0
        and n % 2 == 0
        and frames_local == 1
        and places % n == 0
        and (places // n) % 8 == 0
        and places % 16 == 0
        and width % TILE == 0
        and width >= 2 * TILE
        and width % HEAD_DIM == 0
        and out_columns % 48 == 0
        and qkv_columns % 48 == 0
    )


def solution(mesh):
    in_specs = (
        P(None, ("clips", "frame"), "pix", None),
        P(None, None, ("clips", "frame"), "pix", None),
        P(None, "frame"),
        P(None, "frame"),
        P(),
        P("clips"),
    )
    out_specs = (P(None, ("clips", "frame"), "pix", None), P(None, ("clips", "frame"), "pix", None))

    def local(stream, spatial_qkv, out_weight, qkv_weight, mod_table, timestep):
        args = (stream, spatial_qkv, out_weight, qkv_weight, mod_table, timestep)
        if fits_fused(
            mesh, stream.shape[2], stream.shape[3], out_weight.shape[1], qkv_weight.shape[1], stream.shape[1]
        ):
            return per_device_fused(mesh.shape["frame"], *args)
        return per_device(*args)

    return jax.shard_map(local, mesh=mesh, in_specs=in_specs, out_specs=out_specs, check_vma=False)
```
